32 devices in a mesh: row: 4 (over x, core), col: 8 (over z, y).
Axes of the slice: x: 2, y: 2, z: 4, core: 2. Of those that a mesh axis runs over, the one named last changes fastest.
Arguments:
- rollouts: bfloat16 [2560, 8192], P(('row', 'col')), may hold values from -16 to 16
- lengths: int32 [32, 2], replicated, may hold values from 1 to 79, as said below
- offsets: int32 [32, 2], replicated, may hold values from 0 to 2047, as said below
- norm_gain: float32 [8192], P('row'), may hold values from 0.1 to 1.9
- w_query: bfloat16 [8192, 8192], P('row', 'col'), may hold values from -1 to 1
- w_keyvalue: bfloat16 [8192, 2, 1024], P('row'), may hold values from -2 to 2
- w_out: bfloat16 [8192, 8192], P('col', 'row'), may hold values from -0.0625 to 0.0625
Outputs:
- scored: bfloat16 [2048, 8192], P('col', 'row')
The draws below stay inside these ranges and needn't reach their ends.
Inputs may be any that keep to these rules, and one draw needn't show every extreme that they name: Decode device i holds its rollouts back to back in slots from 0 of its 80 slots; the lengths of one device sum to at most 80, exactly 80 on some device; all lengths sum to 2048. The rollouts cover the positions 0 to 2047 exactly once: rollout k holds offsets[k] to offsets[k] + lengths[k] - 1.
All inputs are finite; a program needn't handle non-finite values.
Results may differ from the reference program's by a relative error of at most 0.013.
The reference program's roundings to bfloat16 on the way (of `packed`, `normed`, `query`, `keyvalue`, `weights` and `attended`) count: a program that leaves them out, or rounds other values in their place, can miss the bound.
Values may be sent and summed in bfloat16 or wider, within the bound.
No kernel may reach another device: no remote copies, remote signals or barrier semaphores. Data moves between devices by JAX's collectives and lax.ppermute only.
A program may use at most 128 MiB of HBM per device.

```python
import math
import jax
import jax.numpy as jnp
from jax import lax

D = 8192
HEADS = 64
KV_HEADS = 8
HEAD_DIM = 128
TOK_COL = 256
RPD = 2
TOKENS = 2048
ROLL_CAP = 80
N_ROW = 4
N_COL = 8
DEVICES = 32


def packing_draw(key):
    key = jax.random.fold_in(key, 101)
    key_delta, key_order, key_cuts, key_place = jax.random.split(key, 4)
    mean_load = TOK_COL // N_ROW
    spread = ROLL_CAP - mean_load
    half_count = DEVICES // 2
    delta = jax.random.randint(key_delta, (half_count,), 0, spread + 1).astype(jnp.int32)
    delta = delta.at[0].set(spread)
    totals = jnp.concatenate([mean_load + delta, mean_load - delta]).astype(jnp.int32)
    upper = (totals - RPD + 1)[:, None]
    cuts = jax.random.randint(key_cuts, (DEVICES, RPD - 1), 0, upper).astype(jnp.int32)
    cuts = cuts.at[0].set(0)
    cuts = jnp.sort(cuts, axis=1)
    edges = jnp.concatenate([jnp.zeros((DEVICES, 1), jnp.int32), cuts, (totals - RPD)[:, None]], axis=1)
    lengths = (1 + edges[:, 1:] - edges[:, :-1]).astype(jnp.int32)
    lengths = lengths[jax.random.permutation(key_order, DEVICES)]
    flat_length = lengths.reshape(-1)
    order = jax.random.permutation(key_place, DEVICES * RPD)
    placed = flat_length[order]
    starts = jnp.cumsum(placed) - placed
    offsets = jnp.zeros((DEVICES * RPD,), jnp.int32).at[order].set(starts.astype(jnp.int32))
    return (lengths, offsets.reshape(DEVICES, RPD))


def query_base(key):
    key = jax.random.fold_in(key, 202)
    values = jax.random.normal(key, (D, HEADS * HEAD_DIM), jnp.float32)
    return jnp.clip(values, -4.0, 4.0) * D ** (-0.5)


def draw_lengths(key, part):
    lengths, offsets = packing_draw(key)
    return lengths


def draw_offsets(key, part):
    lengths, offsets = packing_draw(key)
    return offsets


def draw_w_query(key, part):
    return query_base(key).astype(jnp.bfloat16)


def draw_w_keyvalue(key, part):
    key = jax.random.fold_in(key, 303)
    weights = jnp.clip(jax.random.normal(key, (D, 2, KV_HEADS * HEAD_DIM), jnp.float32), -4.0, 4.0) * D ** (-0.5)
    weights = jnp.clip(weights, -2.0, 2.0)
    return weights.astype(jnp.bfloat16)


def draw_rollouts(key, part):
    key = jax.random.fold_in(key, 404)
    key_main = jax.random.fold_in(key, 0)
    ramp = jnp.exp(math.log(3.0) * jnp.arange(D, dtype=jnp.float32) / (D - 1))
    values = jnp.clip(jax.random.normal(key_main, (DEVICES * ROLL_CAP, D), jnp.float32), -4.0, 4.0) * ramp[None, :]
    return values.astype(jnp.bfloat16)


def shard_levels(own_key, extent, pieces, smallest, high):
    loudness, own = 1.0, jax.random.fold_in(own_key, 6)
    for position, parts in pieces:
        steps = jnp.exp(jax.random.uniform(jax.random.fold_in(own, position), (parts,), jnp.float32, smallest / len(pieces), high / len(pieces)))
        loudness = loudness * jnp.repeat(steps, extent[position] // parts).reshape([-1 if axis == position else 1 for axis in range(len(extent))])
    return loudness


def centred(rng, dims, deviation, most, cuts=(), kind=jnp.bfloat16):
    loudness = shard_levels(rng, dims, cuts, -0.22, 0.18) if cuts else 1.0
    entries = jax.random.normal(rng, dims, jnp.float32) * deviation * loudness
    return jnp.minimum(jnp.maximum(entries, -most), most).astype(kind)


def setup_inputs(seed: int = 0) -> dict:
    seeds = jax.random.split(jax.random.key(seed), 8)
    rollouts = draw_rollouts(jax.random.fold_in(seeds[7], 71), 0)
    lengths = draw_lengths(jax.random.fold_in(seeds[7], 71), 0)
    offsets = draw_offsets(jax.random.fold_in(seeds[7], 71), 0)
    norm_gain = jnp.clip(1.0 + 0.18 * jax.random.normal(seeds[3], (D,), jnp.float32), 0.1, 1.9)
    w_query = draw_w_query(jax.random.fold_in(seeds[7], 71), 0)
    w_keyvalue = draw_w_keyvalue(jax.random.fold_in(seeds[7], 71), 0)
    w_out = centred(seeds[6], (HEADS * HEAD_DIM, D), (HEADS * HEAD_DIM) ** -0.5, 0.0625, ((0, 8), (1, 4)))
    return dict(rollouts=rollouts, lengths=lengths, offsets=offsets, norm_gain=norm_gain, w_query=w_query, w_keyvalue=w_keyvalue, w_out=w_out)


def locate(lengths, offsets):
    local_start = jnp.cumsum(lengths, axis=1) - lengths
    owners = lengths.shape[0]
    slot_start = (jnp.arange(owners, dtype=jnp.int32)[:, None] * ROLL_CAP + local_start).reshape(-1)
    roll_offset = offsets.reshape(-1)
    roll_length = lengths.reshape(-1)
    positions = jnp.arange(TOKENS, dtype=jnp.int32)
    member = ((positions[:, None] >= roll_offset[None, :]) & (positions[:, None] < (roll_offset + roll_length)[None, :])).astype(jnp.int32)
    source = lax.optimization_barrier(jnp.sum(member * (slot_start - roll_offset)[None, :], axis=1)) + positions
    segment = lax.optimization_barrier(jnp.sum(member * jnp.arange(roll_length.shape[0], dtype=jnp.int32)[None, :], axis=1))
    return (source.astype(jnp.int32), segment.astype(jnp.int32))

def reference(rollouts, lengths, offsets, norm_gain, w_query, w_keyvalue, w_out):
    source, segment = locate(lengths, offsets)
    packed = jnp.take(rollouts, source, axis=0)
    values_f = packed.astype(jnp.float32)
    mean_sq = lax.optimization_barrier(jnp.mean(values_f * values_f, axis=1, keepdims=True))
    normed = (values_f * lax.rsqrt(mean_sq + 1e-05) * norm_gain[None, :]).astype(jnp.bfloat16)
    query = jnp.dot(normed, w_query, preferred_element_type=jnp.float32).astype(jnp.bfloat16)
    keyvalue = jnp.dot(normed, w_keyvalue.reshape(D, -1), preferred_element_type=jnp.float32).astype(jnp.bfloat16)
    keys = keyvalue[:, :KV_HEADS * HEAD_DIM].reshape(TOKENS, KV_HEADS, HEAD_DIM).transpose(1, 0, 2)
    values = keyvalue[:, KV_HEADS * HEAD_DIM:].reshape(TOKENS, KV_HEADS, HEAD_DIM).transpose(1, 0, 2)
    positions = jnp.arange(TOKENS, dtype=jnp.int32)
    allowed = (segment[:, None] == segment[None, :]) & (positions[None, :] <= positions[:, None])
    per_head = query.reshape(TOKENS, HEADS, HEAD_DIM).transpose(1, 0, 2)
    group_size = HEADS // KV_HEADS
    kv_index = (jnp.arange(HEADS, dtype=jnp.int32) // group_size).astype(jnp.int32)
    scale = 1.0 / HEAD_DIM ** 0.5

    def one_head(pair):
        q_head, head_kv = pair
        key_head = keys[head_kv]
        value_head = values[head_kv]
        scores = jnp.dot(q_head, key_head.T, preferred_element_type=jnp.float32) * scale
        scores = jnp.where(allowed, scores, jnp.float32(-1e+30))
        top = lax.optimization_barrier(jnp.max(scores, axis=1, keepdims=True))
        expo = jnp.exp(scores - top)
        weights = (expo / lax.optimization_barrier(jnp.sum(expo, axis=1, keepdims=True))).astype(jnp.bfloat16)
        return jnp.dot(weights, value_head, preferred_element_type=jnp.float32).astype(jnp.bfloat16)
    attended = lax.map(one_head, (per_head, kv_index))
    attended = attended.transpose(1, 0, 2).reshape(TOKENS, HEADS * HEAD_DIM)
    group_width = HEADS // N_COL * HEAD_DIM
    groups = attended.reshape(TOKENS, N_COL, group_width).transpose(1, 0, 2)
    weight_groups = w_out.reshape(N_COL, group_width, D)

    def add_group(total, pair):
        attended_group, weight_group = pair
        product = jnp.dot(attended_group, weight_group, preferred_element_type=jnp.float32).astype(jnp.bfloat16)
        product = lax.optimization_barrier(product)
        return (total + product.astype(jnp.float32), None)
    total, unused = lax.scan(add_group, jnp.zeros((TOKENS, D), jnp.float32), (groups, weight_groups))
    return total.astype(jnp.bfloat16)
```

```python
import functools

import jax
import jax.numpy as jnp
from jax import lax
from jax.experimental import pallas as pl
from jax.experimental.pallas import tpu as pltpu
from jax.sharding import PartitionSpec as P

HEADS = 64
KV_HEADS = 8
HEAD_DIM = 128
TOK_COL = 256
F32 = jnp.float32
BF16 = jnp.bfloat16


def locate(lengths, offsets, slot_count, tokens):
    local_start = jnp.cumsum(lengths, axis=1) - lengths
    owners = lengths.shape[0]
    slot_start = jnp.arange(owners, dtype=jnp.int32)[:, None] * slot_count + local_start
    roll_offset = offsets.reshape(-1)
    roll_length = lengths.reshape(-1)
    positions = jnp.arange(tokens, dtype=jnp.int32)
    member = (
        (positions[:, None] >= roll_offset[None, :])
        & (positions[:, None] < (roll_offset + roll_length)[None, :])
    ).astype(jnp.int32)
    return jnp.sum(member * (slot_start.reshape(-1) - roll_offset)[None, :], axis=1) + positions


def attend_kernel(heads, first_ref, *refs):
    *sum_refs, out_ref = refs
    total = sum_refs[0][0]
    for ref in sum_refs[1:]:
        total = total + ref[0].astype(F32)
    qkv = total.astype(BF16).astype(F32)
    slots = qkv.shape[0]
    width = heads * HEAD_DIM
    query = jnp.concatenate(
        [qkv[:, h * HEAD_DIM : (h + 1) * HEAD_DIM] for h in range(heads)], axis=0
    ).astype(BF16)
    keys = qkv[:, width : width + HEAD_DIM].astype(BF16)
    values = qkv[:, width + HEAD_DIM :].astype(BF16)
    first = first_ref[pl.program_id(0)]
    t = lax.broadcasted_iota(jnp.int32, (slots, slots), 0)
    u = lax.broadcasted_iota(jnp.int32, (slots, slots), 1)
    allowed = (u <= t) & ((t < first) == (u < first))
    scores = lax.dot_general(
        query, keys, (((1,), (1,)), ((), ())), preferred_element_type=F32
    ) * (1.0 / HEAD_DIM**0.5)
    scores = jnp.where(allowed[None], scores.reshape(heads, slots, slots), F32(-1e30))
    top = jnp.max(scores, axis=2, keepdims=True)
    expo = jnp.exp(scores - top)
    weights = expo / jnp.sum(expo, axis=2, keepdims=True)
    weights = weights.reshape(heads * slots, slots).astype(BF16)
    out = jnp.dot(weights, values, preferred_element_type=F32)
    out_ref[0] = jnp.concatenate(
        [out[h * slots : (h + 1) * slots] for h in range(heads)], axis=1
    ).astype(BF16)


def attend(first, sums, heads):
    chunks, slots, width = sums[0].shape
    out_width = heads * HEAD_DIM
    return pl.pallas_call(
        functools.partial(attend_kernel, heads),
        grid=(chunks,),
        in_specs=[pl.BlockSpec(memory_space=pltpu.SMEM)]
        + [pl.BlockSpec((1, slots, width), lambda i: (i, 0, 0)) for _ in sums],
        out_specs=pl.BlockSpec((1, slots, out_width), lambda i: (i, 0, 0)),
        out_shape=jax.ShapeDtypeStruct((chunks, slots, out_width), BF16),
        compiler_params=pltpu.CompilerParams(vmem_limit_bytes=32 * 1024 * 1024),
        cost_estimate=pl.CostEstimate(
            flops=4 * chunks * heads * slots * slots * HEAD_DIM,
            bytes_accessed=chunks * slots * width * 10,
            transcendentals=chunks * heads * slots * slots,
        ),
    )(first, *sums)


def ring_order(outer, inner):
    if inner == 1:
        return list(range(outer))
    if inner == 2 or outer % 2:
        order = [z * inner for z in range(outer)]
        for z in reversed(range(outer)):
            step = range(1, inner)
            order += [z * inner + y for y in (step if (outer - 1 - z) % 2 == 0 else reversed(step))]
        return order
    order = [z * inner for z in range(outer)]
    for z in reversed(range(outer)):
        step = range(1, inner)
        order += [z * inner + y for y in (step if (outer - 1 - z) % 2 == 0 else reversed(step))]
    return order


def body(n_row, n_col, rollouts, lengths, offsets, norm_gain, w_query, w_keyvalue, w_out):
    slots, full_width = rollouts.shape
    width = full_width // n_row
    tokens = TOK_COL * n_col
    n_x = n_row // 2
    half = n_col // 2
    heads = w_query.shape[1] // HEAD_DIM
    order = ring_order(n_col // 2, 2) if n_col == 8 else ring_order(4, n_col // 4)
    place = [order.index(c) for c in range(n_col)]
    me_r, me_c = lax.axis_index("row"), lax.axis_index("col")
    me_x, me_k = me_r // 2, me_r % 2
    my_place = jnp.asarray(place, jnp.int32)[me_c]
    order_a = jnp.asarray(order, jnp.int32)

    fwd = [(order[i], order[(i + 1) % n_col]) for i in range(n_col)]
    bwd = [(b, a) for a, b in fwd]

    def row_perm(dx, k):
        return [
            (((x + dx) % n_x) * 2 + (c ^ k), x * 2 + c) for x in range(n_x) for c in range(2)
        ]

    def from_row(value, dx, k):
        return lax.ppermute(value, "row", row_perm(dx, k))

    def to_x(value, dx):
        return lax.ppermute(
            value, "row", [(x * 2 + c, ((x + dx) % n_x) * 2 + c) for x in range(n_x) for c in range(2)]
        )

    raw = rollouts.astype(F32)
    inverse = lax.rsqrt(jnp.sum(raw * raw, axis=1) / full_width + 1e-05)

    def normalise(piece, scale):
        return (piece.astype(F32) * scale[:, None] * norm_gain[None, :]).astype(BF16)

    def features_of(row):
        return lax.dynamic_slice_in_dim(rollouts, row * width, width, 1)

    held = []
    for dx in range(n_x):
        pair = []
        for k in range(2):
            target = ((me_x - dx) % n_x) * 2 + (me_k ^ k)
            piece, scale = features_of(target), inverse
            if dx or k:
                piece, scale = from_row(piece, dx, k), from_row(scale, dx, k)
            pair.append(normalise(piece, scale))
        held.append(jnp.stack(pair))

    kv_head = me_c * heads // (HEADS // KV_HEADS)
    w_kv = lax.dynamic_slice_in_dim(w_keyvalue, kv_head * HEAD_DIM, HEAD_DIM, 2).reshape(width, -1)
    w_all = jnp.concatenate([w_query, w_kv], axis=1)

    groups = [[(0, held)]]
    ahead, behind = list(held), list(held)
    for s in range(1, half):
        ahead = [lax.ppermute(h, "col", fwd) for h in ahead]
        behind = [lax.ppermute(h, "col", bwd) for h in behind]
        groups.append([(n_col - s, ahead), (s, behind)])
    last = [
        lax.ppermute(ahead[dx], "col", fwd) if dx < n_x // 2 else lax.ppermute(behind[dx], "col", bwd)
        for dx in range(n_x)
    ]
    groups.append([(half, last)])

    source = locate(lengths, offsets, slots, tokens)
    owner, slot = source // slots, source % slots
    owner_r, owner_c = owner // n_col, owner % n_col
    far = (jnp.asarray(place, jnp.int32)[owner_c] - my_place) % n_col
    d_x = (owner_r // 2 - me_x) % n_x
    d_k = (owner_r % 2) ^ me_k
    group_of, member_of, base_of, size_of = [0] * n_col, [0] * n_col, [0] * n_col, [0] * n_col
    base, bases = 0, []
    for g, group in enumerate(groups):
        bases.append(base)
        for m, (q, _) in enumerate(group):
            member_of[q], base_of[q], size_of[q] = m, base, len(group)
        base += len(group) * n_row * slots
    table = lambda values: jnp.asarray(values, jnp.int32)[far]
    place_in = (
        table(base_of)
        + ((d_k * table(size_of) + table(member_of)) * n_x + d_x) * slots
        + slot
    )
    dest = order_a[(my_place + jnp.arange(n_col, dtype=jnp.int32)) % n_col]
    place_in = place_in.reshape(n_col, TOK_COL)[dest].reshape(tokens)

    packed = None
    for g, group in enumerate(groups):
        m = len(group)
        rows = jnp.stack([jnp.stack(h, axis=1) for _, h in group], axis=1)
        partial = jnp.dot(
            rows.reshape(2 * m * n_x * slots, width), w_all, preferred_element_type=F32
        ).reshape(2, m, n_x, slots, -1)
        chip = partial[0]
        other = from_row(partial[1], 0, 1)
        sums = [chip[:, 0], other[:, 0]]
        for dx in range(1, n_x):
            sums.append(to_x((chip[:, dx] + other[:, dx]).astype(BF16), dx))
        owners = jnp.stack(
            [me_r * n_col + order_a[(my_place + q) % n_col] for q, _ in group]
        )
        mine = attend(lengths[owners, 0], sums, heads)
        here = jnp.stack([mine] + [from_row(mine, dx, 0) for dx in range(1, n_x)], axis=1)
        there = from_row(here, 0, 1)
        attended = jnp.stack([here, there]).reshape(2 * m * n_x * slots, -1)
        pick = (
            place_in[:, None]
            == (bases[g] + jnp.arange(attended.shape[0], dtype=jnp.int32))[None, :]
        ).astype(BF16)
        placed = jnp.dot(pick, attended, preferred_element_type=F32)
        packed = placed.astype(BF16) if packed is None else (placed + packed.astype(F32)).astype(BF16)

    blocks = packed.reshape(n_col, TOK_COL, -1)
    cols = w_out.shape[1]
    w_parts = [w_out[:, : cols // 2], w_out[:, cols // 2 :]]

    def product(q, part):
        return jnp.dot(blocks[q % n_col], w_parts[part], preferred_element_type=F32)

    send_f, send_b = [None, None], [None, None]
    for q in range(half, 0, -1):
        for part in range(2):
            if q == half and part == 1:
                continue
            value = product(q, part)
            if send_f[part] is not None:
                value = value + send_f[part].astype(F32)
            send_f[part] = lax.ppermute(value.astype(BF16), "col", fwd)
            value = product(-q, 1 - part)
            if send_b[1 - part] is not None:
                value = value + send_b[1 - part].astype(F32)
            send_b[1 - part] = lax.ppermute(value.astype(BF16), "col", bwd)
    final = [
        (product(0, p) + send_f[p].astype(F32) + send_b[p].astype(F32)).astype(BF16) for p in range(2)
    ]
    return jnp.concatenate(final, axis=1)


def solution(mesh):
    in_specs = (
        P(("row", "col"), None),
        P(),
        P(),
        P("row"),
        P("row", "col"),
        P("row", None, None),
        P("col", "row"),
    )
    call = functools.partial(body, mesh.shape["row"], mesh.shape["col"])
    return jax.shard_map(call, mesh=mesh, in_specs=in_specs, out_specs=P("col", "row"), check_vma=False)
```

```python
import functools

import jax
import jax.numpy as jnp
from jax import lax
from jax.experimental import pallas as pl
from jax.experimental.pallas import tpu as pltpu
from jax.sharding import PartitionSpec as P

HEADS = 64
KV_HEADS = 8
HEAD_DIM = 128
TOK_COL = 256
F32 = jnp.float32
BF16 = jnp.bfloat16


def locate(lengths, offsets, slot_count, tokens):
    local_start = jnp.cumsum(lengths, axis=1) - lengths
    owners = lengths.shape[0]
    slot_start = jnp.arange(owners, dtype=jnp.int32)[:, None] * slot_count + local_start
    roll_offset = offsets.reshape(-1)
    roll_length = lengths.reshape(-1)
    positions = jnp.arange(tokens, dtype=jnp.int32)
    member = (
        (positions[:, None] >= roll_offset[None, :])
        & (positions[:, None] < (roll_offset + roll_length)[None, :])
    ).astype(jnp.int32)
    return jnp.sum(member * (slot_start.reshape(-1) - roll_offset)[None, :], axis=1) + positions


def attend_kernel(heads, first_ref, *refs):
    *sum_refs, out_ref = refs
    total = sum_refs[0][0]
    for ref in sum_refs[1:]:
        total = total + ref[0].astype(F32)
    qkv = total.astype(BF16).astype(F32)
    slots = qkv.shape[0]
    width = heads * HEAD_DIM
    query = jnp.concatenate(
        [qkv[:, h * HEAD_DIM : (h + 1) * HEAD_DIM] for h in range(heads)], axis=0
    ).astype(BF16)
    keys = qkv[:, width : width + HEAD_DIM].astype(BF16)
    values = qkv[:, width + HEAD_DIM :].astype(BF16)
    first = first_ref[pl.program_id(0)]
    t = lax.broadcasted_iota(jnp.int32, (slots, slots), 0)
    u = lax.broadcasted_iota(jnp.int32, (slots, slots), 1)
    allowed = (u <= t) & ((t < first) == (u < first))
    scores = lax.dot_general(
        query, keys, (((1,), (1,)), ((), ())), preferred_element_type=F32
    ) * (1.0 / HEAD_DIM**0.5)
    scores = jnp.where(allowed[None], scores.reshape(heads, slots, slots), F32(-1e30))
    top = jnp.max(scores, axis=2, keepdims=True)
    expo = jnp.exp(scores - top)
    weights = expo / jnp.sum(expo, axis=2, keepdims=True)
    weights = weights.reshape(heads * slots, slots).astype(BF16)
    out = jnp.dot(weights, values, preferred_element_type=F32)
    out_ref[0] = jnp.concatenate(
        [out[h * slots : (h + 1) * slots] for h in range(heads)], axis=1
    ).astype(BF16)


def attend(first, sums, heads):
    chunks, slots, width = sums[0].shape
    out_width = heads * HEAD_DIM
    return pl.pallas_call(
        functools.partial(attend_kernel, heads),
        grid=(chunks,),
        in_specs=[pl.BlockSpec(memory_space=pltpu.SMEM)]
        + [pl.BlockSpec((1, slots, width), lambda i: (i, 0, 0)) for _ in sums],
        out_specs=pl.BlockSpec((1, slots, out_width), lambda i: (i, 0, 0)),
        out_shape=jax.ShapeDtypeStruct((chunks, slots, out_width), BF16),
        compiler_params=pltpu.CompilerParams(vmem_limit_bytes=32 * 1024 * 1024),
        cost_estimate=pl.CostEstimate(
            flops=1000,
            bytes_accessed=1000,
            transcendentals=0,
        ),
    )(first, *sums)


def after(value, dep):
    return lax.optimization_barrier((value, dep))[0]


def ring_order(outer, inner):
    if inner == 1:
        return list(range(outer))
    if inner == 2 or outer % 2:
        order = [z * inner for z in range(outer)]
        for z in reversed(range(outer)):
            step = range(1, inner)
            order += [z * inner + y for y in (step if (outer - 1 - z) % 2 == 0 else reversed(step))]
        return order
    order = [z * inner for z in range(outer)]
    for z in reversed(range(outer)):
        step = range(1, inner)
        order += [z * inner + y for y in (step if (outer - 1 - z) % 2 == 0 else reversed(step))]
    return order


def body(n_row, n_col, rollouts, lengths, offsets, norm_gain, w_query, w_keyvalue, w_out):
    slots, full_width = rollouts.shape
    width = full_width // n_row
    tokens = TOK_COL * n_col
    n_x = n_row // 2
    half = n_col // 2
    heads = w_query.shape[1] // HEAD_DIM
    order = ring_order(n_col // 2, 2) if n_col == 8 else ring_order(4, n_col // 4)
    place = [order.index(c) for c in range(n_col)]
    me_r, me_c = lax.axis_index("row"), lax.axis_index("col")
    me_x, me_k = me_r // 2, me_r % 2
    order_a = jnp.asarray(order, jnp.int32)

    fwd = [(order[i], order[(i + 1) % n_col]) for i in range(n_col)]
    bwd = [(b, a) for a, b in fwd]

    def row_perm(dx, k):
        return [
            (((x + dx) % n_x) * 2 + (c ^ k), x * 2 + c) for x in range(n_x) for c in range(2)
        ]

    def from_row(value, dx, k):
        return lax.ppermute(value, "row", row_perm(dx, k))

    def to_x(value, dx):
        return lax.ppermute(
            value, "row", [(x * 2 + c, ((x + dx) % n_x) * 2 + c) for x in range(n_x) for c in range(2)]
        )

    raw = rollouts.astype(F32)
    inverse = lax.rsqrt(jnp.sum(raw * raw, axis=1) / full_width + 1e-05)

    def normalise(piece, scale):
        return (piece.astype(F32) * scale[:, None] * norm_gain[None, :]).astype(BF16)

    def features_of(row):
        return lax.dynamic_slice_in_dim(rollouts, row * width, width, 1)

    arrived_pieces = {
        (dx, k): from_row(features_of(((me_x - dx) % n_x) * 2 + (me_k ^ k)), dx, k)
        for dx in range(n_x)
        for k in range(2)
        if dx or k
    }
    arrived_pieces[0, 0] = features_of(me_r)
    chip_scales = jnp.stack([inverse, from_row(inverse, 0, 1)])
    held = []
    for dx in range(n_x):
        scales = chip_scales
        if dx:
            scales = after(from_row(chip_scales, dx, 0), held[0])
        held.append(jnp.stack([normalise(arrived_pieces[dx, k], scales[k]) for k in range(2)]))
    w_query, w_keyvalue, lengths, offsets, me_r, me_c, norm_gain = after(
        (w_query, w_keyvalue, lengths, offsets, me_r, me_c, norm_gain), held[0]
    )
    me_x, me_k = me_r // 2, me_r % 2
    my_place = jnp.asarray(place, jnp.int32)[me_c]
    kv_head = me_c * heads // (HEADS // KV_HEADS)
    w_kv = lax.dynamic_slice_in_dim(w_keyvalue, kv_head * HEAD_DIM, HEAD_DIM, 2).reshape(width, -1)
    w_all = jnp.concatenate([w_query, w_kv], axis=1)
    owner_first = lengths[:, 0]

    source = locate(lengths, offsets, slots, tokens)
    owner, slot = source // slots, source % slots
    owner_r, owner_c = owner // n_col, owner % n_col
    far = (jnp.asarray(place, jnp.int32)[owner_c] - my_place) % n_col
    d_x = (owner_r // 2 - me_x) % n_x
    d_k = (owner_r % 2) ^ me_k
    kinds = [[0, n_col - 1, 1]] + [[n_col - s, s] for s in range(2, half)] + [[half]]
    member_of, base_of, size_of = [0] * n_col, [0] * n_col, [0] * n_col
    base, bases = 0, []
    for offsets_here in kinds:
        bases.append(base)
        for m, q in enumerate(offsets_here):
            member_of[q], base_of[q], size_of[q] = m, base, len(offsets_here)
        base += len(offsets_here) * n_row * slots
    table = lambda values: jnp.asarray(values, jnp.int32)[far]
    place_in = (
        table(base_of)
        + ((d_k * table(size_of) + table(member_of)) * n_x + d_x) * slots
        + slot
    )
    dest = order_a[(my_place + jnp.arange(n_col, dtype=jnp.int32)) % n_col]
    place_in = place_in.reshape(n_col, TOK_COL)[dest].reshape(tokens)

    def project(group, k, dep):
        rows = jnp.concatenate([h[dx][k] for h in group for dx in range(n_x)], axis=0)
        out = jnp.dot(after(rows, dep), w_all, preferred_element_type=F32)
        return out.reshape(len(group), n_x, slots, -1)

    def work(g, group):
        m = len(group)
        dep = yield
        send = project(group, 1, dep)
        other = from_row(send, 0, 1)
        chip = project(group, 0, send)
        outgoing = [(chip[:, dx] + other[:, dx]).astype(BF16) for dx in range(1, n_x)]
        dep = yield outgoing
        sums = [after(chip[:, 0], dep), other[:, 0]]
        for dx in range(1, n_x):
            sums.append(to_x(outgoing[dx - 1], dx))
        owners = jnp.stack([me_r * n_col + order_a[(my_place + q) % n_col] for q in kinds[g]])
        mine = attend(owner_first[owners], sums, heads)
        dep = yield mine
        here = jnp.stack([mine] + [from_row(mine, dx, 0) for dx in range(1, n_x)], axis=1)
        here = after(here, dep)
        dep = yield here
        there = from_row(here, 0, 1)
        attended = jnp.stack([here, there]).reshape(2 * m * n_x * slots, -1)
        pick = (
            place_in[:, None]
            == (bases[g] + jnp.arange(attended.shape[0], dtype=jnp.int32))[None, :]
        ).astype(BF16)
        placed = jnp.dot(pick, after(attended, dep), preferred_element_type=F32)
        packed[0] = (
            placed.astype(BF16)
            if packed[0] is None
            else (placed + packed[0].astype(F32)).astype(BF16)
        )
        yield packed[0]

    packed = [None]
    running = []

    def begin(g, group):
        running.append(work(g, group))
        next(running[-1])

    def step(index, dep):
        try:
            return running[index].send(dep)
        except StopIteration:
            return None

    ahead, behind, arrived = list(held), list(held), []
    for s in range(1, half):
        ahead = [lax.ppermute(h, "col", fwd) for h in ahead]
        behind = [lax.ppermute(h, "col", bwd) for h in behind]
        arrived.append([ahead, behind])
    last = [
        lax.ppermute(ahead[dx], "col", fwd) if dx < n_x // 2 else lax.ppermute(behind[dx], "col", bwd)
        for dx in range(n_x)
    ]
    begin(0, [held] + arrived[0])
    for g in range(1, half - 1):
        begin(g, arrived[g])
    begin(half - 1, [last])
    turns = []
    for g in range(half):
        for i in range(4):
            turns.append((2 * g + 3 + i - (g >= half - 2), i, g))
    dep = held[0]
    for turn, _, g in sorted(turns, key=lambda v: (v[0], v[2])):
        if turn <= 2 * half - 2:
            there = n_x // 2 * (turn % 2 + 1) - 1
            dep = (dep, [side[there] for side in arrived[(turn - 1) // 2]])
        elif turn == 2 * half - 1:
            dep = (dep, last)
        dep = step(g, dep)
    packed = packed[0]

    blocks = packed.reshape(n_col, TOK_COL, -1)
    cols = w_out.shape[1]
    w_parts = [w_out[:, : cols // 2], w_out[:, cols // 2 :]]

    def product(q, part, more=None):
        block = blocks[q % n_col]
        if more is None:
            return jnp.dot(block, w_parts[part], preferred_element_type=F32)
        block = after(block, more)
        return jnp.dot(block, w_parts[part], preferred_element_type=F32) + more.astype(F32)

    send_f, send_b = [None, None], [None, None]
    for q in range(half, 0, -1):
        for part in range(2):
            if q == half and part == 1:
                continue
            send_f[part] = lax.ppermute(product(q, part, send_f[part]).astype(BF16), "col", fwd)
            back = 1 - part
            send_b[back] = lax.ppermute(product(-q, back, send_b[back]).astype(BF16), "col", bwd)
    final = [
        (product(0, p) + send_f[p].astype(F32) + send_b[p].astype(F32)).astype(BF16) for p in range(2)
    ]
    return jnp.concatenate(final, axis=1)


def solution(mesh):
    in_specs = (
        P(("row", "col"), None),
        P(),
        P(),
        P("row"),
        P("row", "col"),
        P("row", None, None),
        P("col", "row"),
    )
    call = functools.partial(body, mesh.shape["row"], mesh.shape["col"])
    return jax.shard_map(call, mesh=mesh, in_specs=in_specs, out_specs=P("col", "row"), check_vma=False)
```

```python
import functools

import jax
import jax.numpy as jnp
from jax import lax
from jax.experimental import pallas as pl
from jax.experimental.pallas import tpu as pltpu
from jax.sharding import PartitionSpec as P

HEADS = 64
KV_HEADS = 8
HEAD_DIM = 128
TOK_COL = 256
F32 = jnp.float32
BF16 = jnp.bfloat16


def locate(lengths, offsets, slot_count, tokens):
    local_start = jnp.cumsum(lengths, axis=1) - lengths
    owners = lengths.shape[0]
    slot_start = jnp.arange(owners, dtype=jnp.int32)[:, None] * slot_count + local_start
    roll_offset = offsets.reshape(-1)
    roll_length = lengths.reshape(-1)
    positions = jnp.arange(tokens, dtype=jnp.int32)
    member = (
        (positions[:, None] >= roll_offset[None, :])
        & (positions[:, None] < (roll_offset + roll_length)[None, :])
    ).astype(jnp.int32)
    return jnp.sum(member * (slot_start.reshape(-1) - roll_offset)[None, :], axis=1) + positions


def attend_kernel(heads, chunks, first_ref, *refs):
    *sum_refs, out_ref = refs
    slots, columns = sum_refs[0].shape[-2:]
    total = sum_refs[0][...].reshape(slots, columns)
    for ref in sum_refs[1:]:
        total = total + ref[...].reshape(slots, columns).astype(F32)
    qkv = total.astype(BF16).astype(F32)
    width = heads * HEAD_DIM
    query = jnp.concatenate(
        [qkv[:, h * HEAD_DIM : (h + 1) * HEAD_DIM] for h in range(heads)], axis=0
    ).astype(BF16)
    keys = qkv[:, width : width + HEAD_DIM].astype(BF16)
    values = qkv[:, width + HEAD_DIM :].astype(BF16)
    chunk = jnp.int32(chunks[0])
    for m, q in enumerate(chunks):
        chunk = jnp.where(pl.program_id(0) == m, q, chunk)
    first = first_ref[chunk]
    t = lax.broadcasted_iota(jnp.int32, (slots, slots), 0)
    u = lax.broadcasted_iota(jnp.int32, (slots, slots), 1)
    allowed = (u <= t) & ((t < first) == (u < first))
    scores = lax.dot_general(
        query, keys, (((1,), (1,)), ((), ())), preferred_element_type=F32
    ) * (1.0 / HEAD_DIM**0.5)
    scores = jnp.where(allowed[None], scores.reshape(heads, slots, slots), F32(-1e30))
    top = jnp.max(scores, axis=2, keepdims=True)
    expo = jnp.exp(scores - top)
    weights = expo / jnp.sum(expo, axis=2, keepdims=True)
    weights = weights.reshape(heads * slots, slots).astype(BF16)
    out = jnp.dot(weights, values, preferred_element_type=F32)
    out_ref[0] = jnp.concatenate(
        [out[h * slots : (h + 1) * slots] for h in range(heads)], axis=1
    ).astype(BF16)


def attend(first, chunks, heads, chip_sums, which, arrived):
    count, _, slots, columns = chip_sums.shape
    out_width = heads * HEAD_DIM
    return pl.pallas_call(
        functools.partial(attend_kernel, heads, chunks),
        grid=(count,),
        in_specs=[
            pl.BlockSpec(memory_space=pltpu.SMEM),
            pl.BlockSpec((1, 1, slots, columns), lambda i: (i, which, 0, 0)),
        ]
        + [pl.BlockSpec((1, slots, columns), lambda i: (i, 0, 0)) for _ in arrived],
        out_specs=pl.BlockSpec((1, slots, out_width), lambda i: (i, 0, 0)),
        out_shape=jax.ShapeDtypeStruct((count, slots, out_width), BF16),
        compiler_params=pltpu.CompilerParams(vmem_limit_bytes=32 * 1024 * 1024),
        cost_estimate=pl.CostEstimate(flops=1000, bytes_accessed=1000, transcendentals=0),
    )(first, chip_sums, *arrived)


def after(value, dep):
    return lax.optimization_barrier((value, dep))[0]


def ring_order(outer, inner):
    if inner == 1:
        return list(range(outer))
    if inner == 2 or outer % 2:
        order = [z * inner for z in range(outer)]
        for z in reversed(range(outer)):
            step = range(1, inner)
            order += [z * inner + y for y in (step if (outer - 1 - z) % 2 == 0 else reversed(step))]
        return order
    order = [z * inner for z in range(outer)]
    for z in reversed(range(outer)):
        step = range(1, inner)
        order += [z * inner + y for y in (step if (outer - 1 - z) % 2 == 0 else reversed(step))]
    return order


def body(n_row, n_col, rollouts, lengths, offsets, norm_gain, w_query, w_keyvalue, w_out):
    slots, full_width = rollouts.shape
    width = full_width // n_row
    tokens = TOK_COL * n_col
    n_x = n_row // 2
    half, half_x = n_col // 2, n_x // 2
    heads = w_query.shape[1] // HEAD_DIM
    order = ring_order(n_col // 2, 2) if n_col == 8 else ring_order(4, n_col // 4)
    place = [order.index(c) for c in range(n_col)]
    me_r, me_c = lax.axis_index("row"), lax.axis_index("col")
    me_x, me_k = me_r // 2, me_r % 2
    order_a = jnp.asarray(order, jnp.int32)

    fwd = [(order[i], order[(i + 1) % n_col]) for i in range(n_col)]
    bwd = [(b, a) for a, b in fwd]

    def row_perm(dx, k):
        return [
            (((x + dx) % n_x) * 2 + (c ^ k), x * 2 + c) for x in range(n_x) for c in range(2)
        ]

    def from_row(value, dx, k):
        return lax.ppermute(value, "row", row_perm(dx, k))

    def to_x(value, dx):
        return lax.ppermute(
            value, "row", [(x * 2 + c, ((x + dx) % n_x) * 2 + c) for x in range(n_x) for c in range(2)]
        )

    w_other = from_row(w_query, 0, 1)
    gain = jnp.concatenate([norm_gain, from_row(norm_gain, 0, 1)])

    def features_of(x):
        return jnp.concatenate(
            [
                lax.dynamic_slice_in_dim(rollouts, (x * 2 + (me_k ^ k)) * width, width, 1)
                for k in range(2)
            ],
            axis=1,
        )

    def swap_cores(parts):
        pairs = [[2 * x, 2 * x + 1] for x in range(n_x)]
        return lax.all_to_all(parts, "row", 0, 0, axis_index_groups=pairs)

    pieces = [features_of((me_x - dx) % n_x) for dx in range(1, n_x)]
    rollouts = after(rollouts, pieces)
    raw = rollouts.astype(F32)
    inverse = lax.rsqrt(jnp.sum(raw * raw, axis=1) / full_width + 1e-05)
    held = []
    for dx in range(n_x):
        if dx:
            piece, scale = from_row(pieces[dx - 1], dx, 0), from_row(inverse, dx, 0)
            piece, scale = after((piece, scale), held[0])
        else:
            piece, scale = features_of(me_x), inverse
        held.append((piece.astype(F32) * scale[:, None] * gain).astype(BF16))

    kv_head = me_c * heads // (HEADS // KV_HEADS)
    w_kv = lax.dynamic_slice_in_dim(w_keyvalue, kv_head * HEAD_DIM, HEAD_DIM, 2).reshape(width, -1)
    w_kv_other = from_row(after(w_kv, held[0]), 0, 1)
    w_all = jnp.concatenate(
        [
            jnp.concatenate([w_query, w_other], axis=0),
            jnp.concatenate([w_kv, w_kv_other], axis=0),
        ],
        axis=1,
    )
    w_all = lax.optimization_barrier(w_all)

    lengths, offsets, me_r, me_c = after((lengths, offsets, me_r, me_c), held[-1])
    me_x, me_k = me_r // 2, me_r % 2
    my_place = jnp.asarray(place, jnp.int32)[me_c]
    dest = order_a[(my_place + jnp.arange(n_col, dtype=jnp.int32)) % n_col]
    served = (me_x + half_x) % n_x * 2 + me_k
    row_first = lax.dynamic_slice_in_dim(lengths[:, 0], served * n_col, n_col)[dest]

    kinds = [[0]] + [[n_col - s, s] for s in range(1, half)] + [[half]]
    bases, base = [], 0
    for chunks in kinds:
        bases.append(base)
        base += len(chunks) * n_row * slots

    def positions(dep):
        lengths_now, offsets_now = after((lengths, offsets), dep)
        source = locate(lengths_now, offsets_now, slots, tokens)
        owner, slot = source // slots, source % slots
        owner_r, owner_c = owner // n_col, owner % n_col
        far = (jnp.asarray(place, jnp.int32)[owner_c] - my_place) % n_col
        d_x = (owner_r // 2 - half_x - me_x) % n_x
        member_of, base_of, size_of = [0] * n_col, [0] * n_col, [0] * n_col
        for chunks, base in zip(kinds, bases):
            for m, q in enumerate(chunks):
                member_of[q], base_of[q], size_of[q] = m, base, len(chunks)
        for m, q in enumerate(kinds[half - 1] + kinds[half]):
            member_of[q], base_of[q], size_of[q] = m, bases[half - 1], 3
        table = lambda values: jnp.asarray(values, jnp.int32)[far]
        place_in = (
            table(base_of)
            + ((owner_r % 2 * table(size_of) + table(member_of)) * n_x + d_x) * slots
            + slot
        )
        return place_in.reshape(n_col, TOK_COL)[dest].reshape(tokens)

    packed, place_in = [None], [None]

    def work(g, group):
        m = len(group)
        x_type = BF16 if g >= half - 1 else F32
        dep = yield
        rows = jnp.concatenate(after([block for chunk in group for block in chunk], dep))
        rows = lax.optimization_barrier(rows)
        chip = jnp.dot(rows, w_all, preferred_element_type=F32).reshape(m, n_x, slots, -1)
        sums = [
            to_x(chip[:, dx].astype(x_type), (dx + half_x) % n_x)
            for dx in range(n_x)
            if dx != half_x
        ]
        dep = yield chip
        first, chip = after((row_first, chip), dep)
        mine = attend(first, kinds[g], heads, chip, half_x, sums)
        dep = yield mine
        here = jnp.stack([mine] + [from_row(mine, dx, 0) for dx in range(1, n_x)], axis=1)
        here = after(here, dep).reshape(m * n_x * slots, -1)
        if g == half - 1:
            kept.append(here)
            yield here
            return
        if g == half:
            here = jnp.concatenate([kept[0], here])
        rows = here.shape[0]
        attended = swap_cores(jnp.stack([here, here])).reshape(2 * rows, -1)
        number = bases[min(g, half - 1)] + jnp.arange(2 * rows, dtype=jnp.int32)
        pick = (place_in[0][:, None] == number[None, :]).astype(BF16)
        placed = jnp.dot(pick, attended, preferred_element_type=F32)
        if packed[0] is not None:
            placed = placed + packed[0].astype(F32)
        packed[0] = placed.astype(BF16)
        yield packed[0]

    kept = []
    running = [None] * (half + 1)
    latest = [held[-1]]

    def begin(g, group):
        running[g] = work(g, group)
        next(running[g])

    def window(arrival, groups):
        dep = (latest[0], arrival)
        for g in groups:
            dep = running[g].send(dep)
        latest[0] = dep

    ahead = [lax.ppermute(h, "col", fwd) for h in held]
    behind = [lax.ppermute(h, "col", bwd) for h in held]
    begin(0, [held])
    window(held[-1], (0,))
    last = []
    for s in range(1, half):
        begin(s, [ahead, behind])
        next_ahead, next_behind = list(ahead), list(behind)
        for part in range(2):
            dxs = range(part * half_x, (part + 1) * half_x)
            gate = latest[0]
            for dx in dxs:
                front, back = after((ahead[dx], behind[dx]), gate)
                if s < half - 1:
                    next_ahead[dx] = lax.ppermute(front, "col", fwd)
                    next_behind[dx] = lax.ppermute(back, "col", bwd)
                elif part == 0:
                    last.append(lax.ppermute(front, "col", fwd))
                else:
                    last.append(lax.ppermute(back, "col", bwd))
            steps = (max(s - 2, 0),) if part == 0 else (s - 1, s) if s > 1 else (s,)
            window([(ahead[dx], behind[dx]) for dx in dxs], steps)
            if s == 1 and part == 0:
                place_in[0] = positions(latest[0])
            elif s == 1:
                latest[0] = (latest[0], place_in[0])
        ahead, behind = next_ahead, next_behind
    begin(half, [last])
    window(last, (half, half - 2, half - 1, half, half - 1, half))
    packed = packed[0]

    blocks = packed.reshape(n_col, TOK_COL, -1)
    cols = w_out.shape[1]
    w_parts = [w_out[:, : cols // 2], w_out[:, cols // 2 :]]

    def product(q, part, more=None):
        block = blocks[q % n_col]
        if more is not None:
            block = after(block, more)
        out = jnp.dot(block, w_parts[part], preferred_element_type=F32)
        out = lax.reduce_precision(out, 8, 7)
        return out if more is None else out + more.astype(F32)

    send_f, send_b = [None, None], [None, None]
    for q in range(half, 0, -1):
        for part in range(2):
            if q == half and part == 1:
                continue
            send_f[part] = lax.ppermute(product(q, part, send_f[part]).astype(BF16), "col", fwd)
            back = 1 - part
            send_b[back] = lax.ppermute(product(-q, back, send_b[back]).astype(BF16), "col", bwd)
    final = [
        (product(0, p) + send_f[p].astype(F32) + send_b[p].astype(F32)).astype(BF16) for p in range(2)
    ]
    return jnp.concatenate(final, axis=1)


def solution(mesh):
    in_specs = (
        P(("row", "col"), None),
        P(),
        P(),
        P("row"),
        P("row", "col"),
        P("row", None, None),
        P("col", "row"),
    )
    call = functools.partial(body, mesh.shape["row"], mesh.shape["col"])
    return jax.shard_map(call, mesh=mesh, in_specs=in_specs, out_specs=P("col", "row"), check_vma=False)
```

```python
import functools

import jax
import jax.numpy as jnp
from jax import lax
from jax.experimental import pallas as pl
from jax.experimental.pallas import tpu as pltpu
from jax.sharding import PartitionSpec as P

HEADS = 64
KV_HEADS = 8
HEAD_DIM = 128
TOK_COL = 256
F32 = jnp.float32
BF16 = jnp.bfloat16


def locate(lengths, offsets, slot_count, tokens):
    local_start = jnp.cumsum(lengths, axis=1) - lengths
    owners = lengths.shape[0]
    slot_start = jnp.arange(owners, dtype=jnp.int32)[:, None] * slot_count + local_start
    roll_offset = offsets.reshape(-1)
    roll_length = lengths.reshape(-1)
    positions = jnp.arange(tokens, dtype=jnp.int32)
    member = (
        (positions[:, None] >= roll_offset[None, :])
        & (positions[:, None] < (roll_offset + roll_length)[None, :])
    ).astype(jnp.int32)
    return jnp.sum(member * (slot_start.reshape(-1) - roll_offset)[None, :], axis=1) + positions


def attend_kernel(heads, chunks, first_ref, *refs):
    *sum_refs, out_ref = refs
    slots, columns = sum_refs[0].shape[-2:]
    total = sum_refs[0][...].reshape(slots, columns)
    for ref in sum_refs[1:]:
        total = total + ref[...].reshape(slots, columns).astype(F32)
    qkv = total.astype(BF16).astype(F32)
    width = heads * HEAD_DIM
    query = jnp.concatenate(
        [qkv[:, h * HEAD_DIM : (h + 1) * HEAD_DIM] for h in range(heads)], axis=0
    ).astype(BF16)
    keys = qkv[:, width : width + HEAD_DIM].astype(BF16)
    values = qkv[:, width + HEAD_DIM :].astype(BF16)
    chunk = jnp.int32(chunks[0])
    for m, q in enumerate(chunks):
        chunk = jnp.where(pl.program_id(0) == m, q, chunk)
    first = first_ref[chunk]
    t = lax.broadcasted_iota(jnp.int32, (slots, slots), 0)
    u = lax.broadcasted_iota(jnp.int32, (slots, slots), 1)
    allowed = (u <= t) & ((t < first) == (u < first))
    scores = lax.dot_general(
        query, keys, (((1,), (1,)), ((), ())), preferred_element_type=F32
    ) * (1.0 / HEAD_DIM**0.5)
    scores = jnp.where(allowed[None], scores.reshape(heads, slots, slots), F32(-1e30))
    top = jnp.max(scores, axis=2, keepdims=True)
    expo = jnp.exp(scores - top)
    weights = expo / jnp.sum(expo, axis=2, keepdims=True)
    weights = weights.reshape(heads * slots, slots).astype(BF16)
    out = jnp.dot(weights, values, preferred_element_type=F32)
    out_ref[0] = jnp.concatenate(
        [out[h * slots : (h + 1) * slots] for h in range(heads)], axis=1
    ).astype(BF16)


def attend(first, chunks, heads, chip_sums, which, arrived):
    count, _, slots, columns = chip_sums.shape
    out_width = heads * HEAD_DIM
    return pl.pallas_call(
        functools.partial(attend_kernel, heads, chunks),
        grid=(count,),
        in_specs=[
            pl.BlockSpec(memory_space=pltpu.SMEM),
            pl.BlockSpec((1, 1, slots, columns), lambda i: (i, which, 0, 0)),
        ]
        + [pl.BlockSpec((1, slots, columns), lambda i: (i, 0, 0)) for _ in arrived],
        out_specs=pl.BlockSpec((1, slots, out_width), lambda i: (i, 0, 0)),
        out_shape=jax.ShapeDtypeStruct((count, slots, out_width), BF16),
        compiler_params=pltpu.CompilerParams(vmem_limit_bytes=32 * 1024 * 1024),
        cost_estimate=pl.CostEstimate(flops=1000, bytes_accessed=1000, transcendentals=0),
    )(first, chip_sums, *arrived)


def stack_kernel(*refs):
    left_ref, right_ref, out_ref = refs[0], refs[1], refs[-1]
    split = left_ref.shape[1]
    out_ref[:, :split] = left_ref[...]
    out_ref[:, split:] = right_ref[...]


def stack_weights(part, left, right, old):
    rows, columns = left.shape[0], left.shape[1] + right.shape[1]
    tile = rows // 4
    wide = lambda width, base: pl.BlockSpec((tile, width), lambda i: (base + i, 0))
    kept = [] if old is None else [old]
    return pl.pallas_call(
        stack_kernel,
        grid=(4,),
        in_specs=[wide(left.shape[1], 0), wide(right.shape[1], 0)]
        + [pl.BlockSpec(memory_space=pl.ANY)] * len(kept),
        out_specs=wide(columns, 4 * part),
        out_shape=jax.ShapeDtypeStruct((2 * rows, columns), left.dtype),
        input_output_aliases={2: 0} if kept else {},
        compiler_params=pltpu.CompilerParams(vmem_limit_bytes=56 * 1024 * 1024),
        cost_estimate=pl.CostEstimate(flops=1000, bytes_accessed=1000, transcendentals=0),
    )(left, right, *kept)


def after(value, dep):
    return lax.optimization_barrier((value, dep))[0]


def ring_order(outer, inner):
    if inner == 1:
        return list(range(outer))
    if inner == 2 or outer % 2:
        order = [z * inner for z in range(outer)]
        for z in reversed(range(outer)):
            step = range(1, inner)
            order += [z * inner + y for y in (step if (outer - 1 - z) % 2 == 0 else reversed(step))]
        return order
    order = [z * inner for z in range(outer)]
    for z in reversed(range(outer)):
        step = range(1, inner)
        order += [z * inner + y for y in (step if (outer - 1 - z) % 2 == 0 else reversed(step))]
    return order


def body(n_row, n_col, rollouts, lengths, offsets, norm_gain, w_query, w_keyvalue, w_out):
    slots, full_width = rollouts.shape
    width = full_width // n_row
    tokens = TOK_COL * n_col
    n_x = n_row // 2
    half, half_x = n_col // 2, n_x // 2
    heads = w_query.shape[1] // HEAD_DIM
    order = ring_order(n_col // 2, 2) if n_col == 8 else ring_order(4, n_col // 4)
    place = [order.index(c) for c in range(n_col)]
    me_r, me_c = lax.axis_index("row"), lax.axis_index("col")
    me_x, me_k = me_r // 2, me_r % 2
    order_a = jnp.asarray(order, jnp.int32)

    fwd = [(order[i], order[(i + 1) % n_col]) for i in range(n_col)]
    bwd = [(b, a) for a, b in fwd]

    def row_perm(dx, k):
        return [
            (((x + dx) % n_x) * 2 + (c ^ k), x * 2 + c) for x in range(n_x) for c in range(2)
        ]

    def from_row(value, dx, k):
        return lax.ppermute(value, "row", row_perm(dx, k))

    def to_x(value, dx):
        return lax.ppermute(
            value, "row", [(x * 2 + c, ((x + dx) % n_x) * 2 + c) for x in range(n_x) for c in range(2)]
        )

    w_other = from_row(w_query, 0, 1)
    gain = jnp.concatenate([norm_gain, from_row(norm_gain, 0, 1)])

    def features_of(x):
        return jnp.concatenate(
            [
                lax.dynamic_slice_in_dim(rollouts, (x * 2 + (me_k ^ k)) * width, width, 1)
                for k in range(2)
            ],
            axis=1,
        )

    def swap_cores(parts):
        pairs = [[2 * x, 2 * x + 1] for x in range(n_x)]
        return lax.all_to_all(parts, "row", 0, 0, axis_index_groups=pairs)

    pieces = [features_of((me_x - dx) % n_x) for dx in range(1, n_x)]
    rollouts = after(rollouts, pieces)
    raw = rollouts.astype(F32)
    inverse = lax.rsqrt(jnp.sum(raw * raw, axis=1) / full_width + 1e-05)
    held = []
    for dx in range(n_x):
        if dx:
            piece, scale = from_row(pieces[dx - 1], dx, 0), from_row(inverse, dx, 0)
            piece, scale = after((piece, scale), held[0])
        else:
            piece, scale = features_of(me_x), inverse
        held.append((piece.astype(F32) * scale[:, None] * gain).astype(BF16))

    kv_head = me_c * heads // (HEADS // KV_HEADS)
    w_kv = lax.dynamic_slice_in_dim(w_keyvalue, kv_head * HEAD_DIM, HEAD_DIM, 2).reshape(width, -1)
    w_kv_other = from_row(after(w_kv, held[0]), 0, 1)
    w_all = stack_weights(0, w_query, after(w_kv, held[-1]), None)
    w_all = stack_weights(1, w_other, w_kv_other, w_all)

    lengths, offsets, me_r, me_c = after((lengths, offsets, me_r, me_c), held[-1])
    me_x, me_k = me_r // 2, me_r % 2
    my_place = jnp.asarray(place, jnp.int32)[me_c]
    dest = order_a[(my_place + jnp.arange(n_col, dtype=jnp.int32)) % n_col]
    served = (me_x + half_x) % n_x * 2 + me_k
    row_first = lax.dynamic_slice_in_dim(lengths[:, 0], served * n_col, n_col)[dest]

    kinds = [[0]] + [[n_col - s, s] for s in range(1, half)] + [[half]]
    bases, base = [], 0
    for chunks in kinds:
        bases.append(base)
        base += len(chunks) * n_row * slots

    def positions(dep):
        lengths_now, offsets_now = after((lengths, offsets), dep)
        source = locate(lengths_now, offsets_now, slots, tokens)
        owner, slot = source // slots, source % slots
        owner_r, owner_c = owner // n_col, owner % n_col
        far = (jnp.asarray(place, jnp.int32)[owner_c] - my_place) % n_col
        d_x = (owner_r // 2 - half_x - me_x) % n_x
        member_of, base_of, size_of, last_of = ([0] * n_col for _ in range(4))
        for chunks, base in zip(kinds, bases):
            for m, q in enumerate(chunks):
                member_of[q], base_of[q], size_of[q] = m, base, len(chunks)
        for m, q in enumerate(kinds[half - 1] + kinds[half]):
            member_of[q], base_of[q], size_of[q], last_of[q] = m, bases[half - 1], 3, 1
        table = lambda values: jnp.asarray(values, jnp.int32)[far]
        core = jnp.where(table(last_of) == 1, (owner_r % 2) ^ me_k, owner_r % 2)
        place_in = (
            table(base_of)
            + ((core * table(size_of) + table(member_of)) * n_x + d_x) * slots
            + slot
        )
        return place_in.reshape(n_col, TOK_COL)[dest].reshape(tokens)

    packed, place_in = [None], [None]

    def work(g, group):
        m = len(group)
        x_type = BF16 if g == half - 1 else F32
        dep = yield
        rows = jnp.concatenate(after([block for chunk in group for block in chunk], dep))
        rows = lax.optimization_barrier(rows)
        chip = jnp.dot(rows, w_all, preferred_element_type=F32).reshape(m, n_x, slots, -1)
        sums = [
            to_x(chip[:, dx].astype(x_type), (dx + half_x) % n_x)
            for dx in range(n_x)
            if dx != half_x
        ]
        dep = yield chip
        first, chip = after((row_first, chip), dep)
        mine = attend(first, kinds[g], heads, chip, half_x, sums)
        dep = yield mine
        here = jnp.stack([mine] + [from_row(mine, dx, 0) for dx in range(1, n_x)], axis=1)
        here = after(here, dep).reshape(m * n_x * slots, -1)
        if g == half - 1:
            kept.append(here)
            yield here
            return
        if g == half:
            here = jnp.concatenate([kept[0], here])
        rows = here.shape[0]
        if g == half:
            parts = [here, from_row(here, 0, 1)]
        else:
            parts = [swap_cores(jnp.stack([here, here])).reshape(2 * rows, -1)]
        number, placed = bases[min(g, half - 1)], packed[0]
        for part in parts:
            pick = place_in[0][:, None] == number + jnp.arange(part.shape[0], dtype=jnp.int32)[None, :]
            number += part.shape[0]
            more = jnp.dot(pick.astype(BF16), part, preferred_element_type=F32)
            placed = (more if placed is None else more + placed.astype(F32)).astype(BF16)
        packed[0] = placed
        yield packed[0]

    kept = []
    running = [None] * (half + 1)
    latest = [held[-1]]

    def begin(g, group):
        running[g] = work(g, group)
        next(running[g])

    def window(arrival, groups):
        dep = (latest[0], arrival)
        for g in groups:
            dep = running[g].send(dep)
        latest[0] = dep

    ahead = [lax.ppermute(h, "col", fwd) for h in held]
    behind = [lax.ppermute(h, "col", bwd) for h in held]
    begin(0, [held])
    window(held[-1], (0,))
    last = []
    for s in range(1, half):
        begin(s, [ahead, behind])
        next_ahead, next_behind = list(ahead), list(behind)
        for part in range(2):
            dxs = range(part * half_x, (part + 1) * half_x)
            gate = latest[0]
            for dx in dxs:
                front, back = after((ahead[dx], behind[dx]), gate)
                if s < half - 1:
                    next_ahead[dx] = lax.ppermute(front, "col", fwd)
                    next_behind[dx] = lax.ppermute(back, "col", bwd)
                elif part == 0:
                    last.append(lax.ppermute(front, "col", fwd))
                else:
                    last.append(lax.ppermute(back, "col", bwd))
            if part == 0:
                steps = (max(s - 2, 0),)
            else:
                steps = (s - 1, s) if s > 1 else (s,)
            window([(ahead[dx], behind[dx]) for dx in dxs], steps)
            if s == 1 and part == 0:
                place_in[0] = positions(latest[0])
            elif s == 1:
                latest[0] = (latest[0], place_in[0])
        ahead, behind = next_ahead, next_behind
    begin(half, [last])
    window(last, (half, half - 1, half, half - 2, half - 1, half))
    packed = packed[0]

    blocks = packed.reshape(n_col, TOK_COL, -1)
    cols = w_out.shape[1]
    w_parts = [w_out[:, : cols // 2], w_out[:, cols // 2 :]]

    def product(q, part, more=None):
        block = blocks[q % n_col]
        if more is not None:
            block = after(block, more)
        out = jnp.dot(block, w_parts[part], preferred_element_type=F32)
        out = lax.reduce_precision(out, 8, 7)
        return out if more is None else out + more.astype(F32)

    send_f, send_b = [None, None], [None, None]
    for q in range(half, 0, -1):
        for part in range(2):
            if q == half and part == 1:
                continue
            send_f[part] = lax.ppermute(product(q, part, send_f[part]).astype(BF16), "col", fwd)
            back = 1 - part
            send_b[back] = lax.ppermute(product(-q, back, send_b[back]).astype(BF16), "col", bwd)
    final = [
        (product(0, p) + send_f[p].astype(F32) + send_b[p].astype(F32)).astype(BF16) for p in range(2)
    ]
    return jnp.concatenate(final, axis=1)


def solution(mesh):
    in_specs = (
        P(("row", "col"), None),
        P(),
        P(),
        P("row"),
        P("row", "col"),
        P("row", None, None),
        P("col", "row"),
    )
    call = functools.partial(body, mesh.shape["row"], mesh.shape["col"])
    return jax.shard_map(call, mesh=mesh, in_specs=in_specs, out_specs=P("col", "row"), check_vma=False)
```

```python
import functools

import jax
import jax.numpy as jnp
from jax import lax
from jax.experimental import pallas as pl
from jax.experimental.pallas import tpu as pltpu
from jax.sharding import PartitionSpec as P

HEADS = 64
KV_HEADS = 8
HEAD_DIM = 128
TOK_COL = 256
F32 = jnp.float32
BF16 = jnp.bfloat16


def locate(lengths, offsets, slot_count, tokens):
    local_start = jnp.cumsum(lengths, axis=1) - lengths
    owners = lengths.shape[0]
    slot_start = jnp.arange(owners, dtype=jnp.int32)[:, None] * slot_count + local_start
    roll_offset = offsets.reshape(-1)
    roll_length = lengths.reshape(-1)
    positions = jnp.arange(tokens, dtype=jnp.int32)
    member = (
        (positions[:, None] >= roll_offset[None, :])
        & (positions[:, None] < (roll_offset + roll_length)[None, :])
    ).astype(jnp.int32)
    return jnp.sum(member * (slot_start.reshape(-1) - roll_offset)[None, :], axis=1) + positions


def attend_kernel(heads, chunks, first_ref, *refs):
    *sum_refs, out_ref = refs
    slots, columns = sum_refs[0].shape[-2:]
    total = sum_refs[0][...].reshape(slots, columns)
    for ref in sum_refs[1:]:
        total = total + ref[...].reshape(slots, columns).astype(F32)
    qkv = total.astype(BF16).astype(F32)
    width = heads * HEAD_DIM
    query = jnp.concatenate(
        [qkv[:, h * HEAD_DIM : (h + 1) * HEAD_DIM] for h in range(heads)], axis=0
    ).astype(BF16)
    keys = qkv[:, width : width + HEAD_DIM].astype(BF16)
    values = qkv[:, width + HEAD_DIM :].astype(BF16)
    chunk = jnp.int32(chunks[0])
    for m, q in enumerate(chunks):
        chunk = jnp.where(pl.program_id(0) == m, q, chunk)
    first = first_ref[chunk]
    t = lax.broadcasted_iota(jnp.int32, (slots, slots), 0)
    u = lax.broadcasted_iota(jnp.int32, (slots, slots), 1)
    allowed = (u <= t) & ((t < first) == (u < first))
    scores = lax.dot_general(
        query, keys, (((1,), (1,)), ((), ())), preferred_element_type=F32
    ) * (1.0 / HEAD_DIM**0.5)
    scores = jnp.where(allowed[None], scores.reshape(heads, slots, slots), F32(-1e30))
    top = jnp.max(scores, axis=2, keepdims=True)
    expo = jnp.exp(scores - top)
    weights = expo / jnp.sum(expo, axis=2, keepdims=True)
    weights = weights.reshape(heads * slots, slots).astype(BF16)
    out = jnp.dot(weights, values, preferred_element_type=F32)
    out_ref[0] = jnp.concatenate(
        [out[h * slots : (h + 1) * slots] for h in range(heads)], axis=1
    ).astype(BF16)


def attend(first, chunks, heads, chip_sums, which, arrived):
    count, _, slots, columns = chip_sums.shape
    out_width = heads * HEAD_DIM
    return pl.pallas_call(
        functools.partial(attend_kernel, heads, chunks),
        grid=(count,),
        in_specs=[
            pl.BlockSpec(memory_space=pltpu.SMEM),
            pl.BlockSpec((1, 1, slots, columns), lambda i: (i, which, 0, 0)),
        ]
        + [pl.BlockSpec((1, slots, columns), lambda i: (i, 0, 0)) for _ in arrived],
        out_specs=pl.BlockSpec((1, slots, out_width), lambda i: (i, 0, 0)),
        out_shape=jax.ShapeDtypeStruct((count, slots, out_width), BF16),
        compiler_params=pltpu.CompilerParams(vmem_limit_bytes=32 * 1024 * 1024),
        cost_estimate=pl.CostEstimate(flops=1000, bytes_accessed=1000, transcendentals=0),
    )(first, chip_sums, *arrived)


def stack_kernel(*refs):
    left_ref, right_ref, out_ref = refs[0], refs[1], refs[-1]
    split = left_ref.shape[1]
    out_ref[:, :split] = left_ref[...]
    out_ref[:, split:] = right_ref[...]


def stack_weights(part, left, right, old):
    rows, columns = left.shape[0], left.shape[1] + right.shape[1]
    tile = rows // 4
    wide = lambda width, base: pl.BlockSpec((tile, width), lambda i: (base + i, 0))
    kept = [] if old is None else [old]
    return pl.pallas_call(
        stack_kernel,
        grid=(4,),
        in_specs=[wide(left.shape[1], 0), wide(right.shape[1], 0)]
        + [pl.BlockSpec(memory_space=pl.ANY)] * len(kept),
        out_specs=wide(columns, 4 * part),
        out_shape=jax.ShapeDtypeStruct((2 * rows, columns), left.dtype),
        input_output_aliases={2: 0} if kept else {},
        compiler_params=pltpu.CompilerParams(vmem_limit_bytes=56 * 1024 * 1024),
        cost_estimate=pl.CostEstimate(flops=1000, bytes_accessed=1000, transcendentals=0),
    )(left, right, *kept)


def after(value, dep):
    return lax.optimization_barrier((value, dep))[0]


def ring_order(outer, inner):
    if inner == 1:
        return list(range(outer))
    if inner == 2 or outer % 2:
        order = [z * inner for z in range(outer)]
        for z in reversed(range(outer)):
            step = range(1, inner)
            order += [z * inner + y for y in (step if (outer - 1 - z) % 2 == 0 else reversed(step))]
        return order
    order = [z * inner for z in range(outer)]
    for z in reversed(range(outer)):
        step = range(1, inner)
        order += [z * inner + y for y in (step if (outer - 1 - z) % 2 == 0 else reversed(step))]
    return order


def body(n_row, n_col, rollouts, lengths, offsets, norm_gain, w_query, w_keyvalue, w_out):
    slots, full_width = rollouts.shape
    width = full_width // n_row
    tokens = TOK_COL * n_col
    n_x = n_row // 2
    half, half_x = n_col // 2, n_x // 2
    heads = w_query.shape[1] // HEAD_DIM
    order = ring_order(n_col // 2, 2) if n_col == 8 else ring_order(4, n_col // 4)
    place = [order.index(c) for c in range(n_col)]
    me_r, me_c = lax.axis_index("row"), lax.axis_index("col")
    me_x, me_k = me_r // 2, me_r % 2
    order_a = jnp.asarray(order, jnp.int32)

    fwd = [(order[i], order[(i + 1) % n_col]) for i in range(n_col)]
    bwd = [(b, a) for a, b in fwd]

    def row_perm(dx, k):
        return [
            (((x + dx) % n_x) * 2 + (c ^ k), x * 2 + c) for x in range(n_x) for c in range(2)
        ]

    def from_row(value, dx, k):
        return lax.ppermute(value, "row", row_perm(dx, k))

    def to_x(value, dx):
        return lax.ppermute(
            value, "row", [(x * 2 + c, ((x + dx) % n_x) * 2 + c) for x in range(n_x) for c in range(2)]
        )

    w_other = from_row(w_query, 0, 1)
    gain = jnp.concatenate([norm_gain, from_row(norm_gain, 0, 1)])

    def features_of(x):
        return jnp.concatenate(
            [
                lax.dynamic_slice_in_dim(rollouts, (x * 2 + (me_k ^ k)) * width, width, 1)
                for k in range(2)
            ],
            axis=1,
        )

    def swap_cores(parts):
        pairs = [[2 * x, 2 * x + 1] for x in range(n_x)]
        return lax.all_to_all(parts, "row", 0, 0, axis_index_groups=pairs)

    pieces = [features_of((me_x - dx) % n_x) for dx in range(1, n_x)]
    rollouts = after(rollouts, pieces)
    raw = rollouts.astype(F32)
    inverse = lax.rsqrt(jnp.sum(raw * raw, axis=1) / full_width + 1e-05)
    held = []
    for dx in range(n_x):
        if dx:
            piece, scale = from_row(pieces[dx - 1], dx, 0), from_row(inverse, dx, 0)
            piece, scale = after((piece, scale), held[0])
        else:
            piece, scale = features_of(me_x), inverse
        held.append((piece.astype(F32) * scale[:, None] * gain).astype(BF16))

    kv_head = me_c * heads // (HEADS // KV_HEADS)
    w_kv = lax.dynamic_slice_in_dim(w_keyvalue, kv_head * HEAD_DIM, HEAD_DIM, 2).reshape(width, -1)
    w_kv_other = from_row(after(w_kv, held[-1]), 0, 1)
    w_all = stack_weights(0, w_query, after(w_kv, held[-1]), None)
    w_all = stack_weights(1, w_other, w_kv_other, w_all)

    lengths, offsets, me_r, me_c = after((lengths, offsets, me_r, me_c), held[-1])
    me_x, me_k = me_r // 2, me_r % 2
    my_place = jnp.asarray(place, jnp.int32)[me_c]
    dest = order_a[(my_place + jnp.arange(n_col, dtype=jnp.int32)) % n_col]
    served = (me_x + half_x) % n_x * 2 + me_k
    row_first = lax.dynamic_slice_in_dim(lengths[:, 0], served * n_col, n_col)[dest]

    kinds = [[0]] + [[n_col - s, s] for s in range(1, half)] + [[half]]
    bases, base = [], 0
    for chunks in kinds:
        bases.append(base)
        base += len(chunks) * n_row * slots

    def positions(dep):
        lengths_now, offsets_now = after((lengths, offsets), dep)
        source = locate(lengths_now, offsets_now, slots, tokens)
        owner, slot = source // slots, source % slots
        owner_r, owner_c = owner // n_col, owner % n_col
        far = (jnp.asarray(place, jnp.int32)[owner_c] - my_place) % n_col
        d_x = (owner_r // 2 - half_x - me_x) % n_x
        member_of, base_of, size_of, last_of = ([0] * n_col for _ in range(4))
        for chunks, base in zip(kinds, bases):
            for m, q in enumerate(chunks):
                member_of[q], base_of[q], size_of[q] = m, base, len(chunks)
        for m, q in enumerate(kinds[half - 1] + kinds[half]):
            member_of[q], base_of[q], size_of[q], last_of[q] = m, bases[half - 1], 3, 1
        table = lambda values: jnp.asarray(values, jnp.int32)[far]
        core = jnp.where(table(last_of) == 1, (owner_r % 2) ^ me_k, owner_r % 2)
        place_in = (
            table(base_of)
            + ((core * table(size_of) + table(member_of)) * n_x + d_x) * slots
            + slot
        )
        return place_in.reshape(n_col, TOK_COL)[dest].reshape(tokens)

    packed, place_in = [None], [None]

    def work(g, group):
        m = len(group)
        x_type = BF16 if g == half - 1 else F32
        dep = yield
        rows = jnp.concatenate(after([block for chunk in group for block in chunk], dep))
        rows = lax.optimization_barrier(rows)
        chip = jnp.dot(rows, w_all, preferred_element_type=F32).reshape(m, n_x, slots, -1)
        sums = [
            to_x(chip[:, dx].astype(x_type), (dx + half_x) % n_x)
            for dx in range(n_x)
            if dx != half_x
        ]
        dep = yield chip
        first, chip = after((row_first, chip), dep)
        mine = attend(first, kinds[g], heads, chip, half_x, sums)
        dep = yield mine
        here = jnp.stack([mine] + [from_row(mine, dx, 0) for dx in range(1, n_x)], axis=1)
        here = after(here, dep).reshape(m * n_x * slots, -1)
        if g == half - 1:
            kept.append(here)
            yield here
            return
        if g == half:
            here = jnp.concatenate([kept[0], here])
        rows = here.shape[0]
        if g == half:
            parts = [here, from_row(here, 0, 1)]
        else:
            parts = [swap_cores(jnp.stack([here, here])).reshape(2 * rows, -1)]
        number, placed = bases[min(g, half - 1)], packed[0]
        for part in parts:
            pick = place_in[0][:, None] == number + jnp.arange(part.shape[0], dtype=jnp.int32)[None, :]
            number += part.shape[0]
            more = jnp.dot(pick.astype(BF16), part, preferred_element_type=F32)
            placed = (more if placed is None else more + placed.astype(F32)).astype(BF16)
        packed[0] = placed
        yield packed[0]

    kept = []
    running = [None] * (half + 1)
    latest = [held[-1]]

    def begin(g, group):
        running[g] = work(g, group)
        next(running[g])

    def window(arrival, groups):
        dep = (latest[0], arrival)
        for g in groups:
            dep = running[g].send(dep)
        latest[0] = dep

    ahead = [lax.ppermute(h, "col", fwd) for h in held]
    behind = [lax.ppermute(h, "col", bwd) for h in held]
    begin(0, [held])
    window(held[-1], (0,))
    last = []
    for s in range(1, half):
        begin(s, [ahead, behind])
        next_ahead, next_behind = list(ahead), list(behind)
        for part in range(2):
            dxs = range(part * half_x, (part + 1) * half_x)
            gate = latest[0] if s > 1 or part else held[-1]
            for dx in dxs:
                front, back = after((ahead[dx], behind[dx]), gate)
                if s < half - 1:
                    next_ahead[dx] = lax.ppermute(front, "col", fwd)
                    next_behind[dx] = lax.ppermute(back, "col", bwd)
                elif part == 0:
                    last.append(lax.ppermute(front, "col", fwd))
                else:
                    last.append(lax.ppermute(back, "col", bwd))
            if part == 0:
                steps = (s - 2,) if s > 1 else ()
            else:
                steps = (s - 1, s)
            window([(ahead[dx], behind[dx]) for dx in dxs], steps)
            if s == 1 and part == 0:
                place_in[0] = positions(latest[0])
            elif s == 1:
                latest[0] = (latest[0], place_in[0])
        ahead, behind = next_ahead, next_behind
    begin(half, [last])
    window(last, (half, half - 1, half, half - 2, half - 1, half))
    packed = packed[0]

    blocks = packed.reshape(n_col, TOK_COL, -1)
    cols = w_out.shape[1]
    w_parts = [w_out[:, : cols // 2], w_out[:, cols // 2 :]]

    def product(q, part, more=None):
        block = blocks[q % n_col]
        if more is not None:
            block = after(block, more)
        out = jnp.dot(block, w_parts[part], preferred_element_type=F32)
        out = lax.reduce_precision(out, 8, 7)
        return out if more is None else out + more.astype(F32)

    send_f, send_b = [None, None], [None, None]
    for q in range(half, 0, -1):
        for part in range(2):
            if q == half and part == 1:
                continue
            send_f[part] = lax.ppermute(product(q, part, send_f[part]).astype(BF16), "col", fwd)
            back = 1 - part
            send_b[back] = lax.ppermute(product(-q, back, send_b[back]).astype(BF16), "col", bwd)
    final = [
        (product(0, p) + send_f[p].astype(F32) + send_b[p].astype(F32)).astype(BF16) for p in range(2)
    ]
    return jnp.concatenate(final, axis=1)


def solution(mesh):
    in_specs = (
        P(("row", "col"), None),
        P(),
        P(),
        P("row"),
        P("row", "col"),
        P("row", None, None),
        P("col", "row"),
    )
    call = functools.partial(body, mesh.shape["row"], mesh.shape["col"])
    return jax.shard_map(call, mesh=mesh, in_specs=in_specs, out_specs=P("col", "row"), check_vma=False)
```

```python
import functools

import jax
import jax.numpy as jnp
from jax import lax
from jax.experimental import pallas as pl
from jax.experimental.pallas import tpu as pltpu
from jax.sharding import PartitionSpec as P

HEADS = 64
KV_HEADS = 8
HEAD_DIM = 128
TOK_COL = 256
F32 = jnp.float32
BF16 = jnp.bfloat16


def locate(lengths, offsets, slot_count, tokens):
    local_start = jnp.cumsum(lengths, axis=1) - lengths
    owners = lengths.shape[0]
    slot_start = jnp.arange(owners, dtype=jnp.int32)[:, None] * slot_count + local_start
    roll_offset = offsets.reshape(-1)
    roll_length = lengths.reshape(-1)
    positions = jnp.arange(tokens, dtype=jnp.int32)
    member = (
        (positions[:, None] >= roll_offset[None, :])
        & (positions[:, None] < (roll_offset + roll_length)[None, :])
    ).astype(jnp.int32)
    return jnp.sum(member * (slot_start.reshape(-1) - roll_offset)[None, :], axis=1) + positions


def attend_kernel(heads, chunks, first_ref, *refs):
    *sum_refs, out_ref = refs
    slots, columns = sum_refs[0].shape[-2:]
    total = sum_refs[0][...].reshape(slots, columns)
    for ref in sum_refs[1:]:
        total = total + ref[...].reshape(slots, columns).astype(F32)
    qkv = total.astype(BF16).astype(F32)
    width = heads * HEAD_DIM
    query = jnp.concatenate(
        [qkv[:, h * HEAD_DIM : (h + 1) * HEAD_DIM] for h in range(heads)], axis=0
    ).astype(BF16)
    keys = qkv[:, width : width + HEAD_DIM].astype(BF16)
    values = qkv[:, width + HEAD_DIM :].astype(BF16)
    chunk = jnp.int32(chunks[0])
    for m, q in enumerate(chunks):
        chunk = jnp.where(pl.program_id(0) == m, q, chunk)
    first = first_ref[chunk]
    t = lax.broadcasted_iota(jnp.int32, (slots, slots), 0)
    u = lax.broadcasted_iota(jnp.int32, (slots, slots), 1)
    allowed = (u <= t) & ((t < first) == (u < first))
    scores = lax.dot_general(
        query, keys, (((1,), (1,)), ((), ())), preferred_element_type=F32
    ) * (1.0 / HEAD_DIM**0.5)
    scores = jnp.where(allowed[None], scores.reshape(heads, slots, slots), F32(-1e30))
    top = jnp.max(scores, axis=2, keepdims=True)
    expo = jnp.exp(scores - top)
    weights = expo / jnp.sum(expo, axis=2, keepdims=True)
    weights = weights.reshape(heads * slots, slots).astype(BF16)
    out = jnp.dot(weights, values, preferred_element_type=F32)
    out_ref[0] = jnp.concatenate(
        [out[h * slots : (h + 1) * slots] for h in range(heads)], axis=1
    ).astype(BF16)


def attend(first, chunks, heads, chip_sums, which, arrived):
    count, _, slots, columns = chip_sums.shape
    out_width = heads * HEAD_DIM
    return pl.pallas_call(
        functools.partial(attend_kernel, heads, chunks),
        grid=(count,),
        in_specs=[
            pl.BlockSpec(memory_space=pltpu.SMEM),
            pl.BlockSpec((1, 1, slots, columns), lambda i: (i, which, 0, 0)),
        ]
        + [pl.BlockSpec((1, slots, columns), lambda i: (i, 0, 0)) for _ in arrived],
        out_specs=pl.BlockSpec((1, slots, out_width), lambda i: (i, 0, 0)),
        out_shape=jax.ShapeDtypeStruct((count, slots, out_width), BF16),
        compiler_params=pltpu.CompilerParams(vmem_limit_bytes=32 * 1024 * 1024),
        cost_estimate=pl.CostEstimate(flops=1000, bytes_accessed=1000, transcendentals=0),
    )(first, chip_sums, *arrived)


def stack_kernel(*refs):
    left_ref, right_ref, out_ref = refs[0], refs[1], refs[-1]
    split = left_ref.shape[1]
    out_ref[:, :split] = left_ref[...]
    out_ref[:, split:] = right_ref[...]


def stack_weights(part, left, right, old):
    rows, columns = left.shape[0], left.shape[1] + right.shape[1]
    tile = rows // 4
    wide = lambda width, base: pl.BlockSpec((tile, width), lambda i: (base + i, 0))
    kept = [] if old is None else [old]
    return pl.pallas_call(
        stack_kernel,
        grid=(4,),
        in_specs=[wide(left.shape[1], 0), wide(right.shape[1], 0)]
        + [pl.BlockSpec(memory_space=pl.ANY)] * len(kept),
        out_specs=wide(columns, 4 * part),
        out_shape=jax.ShapeDtypeStruct((2 * rows, columns), left.dtype),
        input_output_aliases={2: 0} if kept else {},
        compiler_params=pltpu.CompilerParams(vmem_limit_bytes=56 * 1024 * 1024),
        cost_estimate=pl.CostEstimate(flops=1000, bytes_accessed=1000, transcendentals=0),
    )(left, right, *kept)


def after(value, dep):
    return lax.optimization_barrier((value, dep))[0]


def ring_order(outer, inner):
    if inner == 1:
        return list(range(outer))
    if inner == 2 or outer % 2:
        order = [z * inner for z in range(outer)]
        for z in reversed(range(outer)):
            step = range(1, inner)
            order += [z * inner + y for y in (step if (outer - 1 - z) % 2 == 0 else reversed(step))]
        return order
    order = [z * inner for z in range(outer)]
    for z in reversed(range(outer)):
        step = range(1, inner)
        order += [z * inner + y for y in (step if (outer - 1 - z) % 2 == 0 else reversed(step))]
    return order


def body(n_row, n_col, rollouts, lengths, offsets, norm_gain, w_query, w_keyvalue, w_out):
    slots, full_width = rollouts.shape
    width = full_width // n_row
    tokens = TOK_COL * n_col
    n_x = n_row // 2
    half, half_x = n_col // 2, n_x // 2
    heads = w_query.shape[1] // HEAD_DIM
    order = ring_order(n_col // 2, 2) if n_col == 8 else ring_order(4, n_col // 4)
    place = [order.index(c) for c in range(n_col)]
    me_r, me_c = lax.axis_index("row"), lax.axis_index("col")
    me_x, me_k = me_r // 2, me_r % 2
    order_a = jnp.asarray(order, jnp.int32)

    fwd = [(order[i], order[(i + 1) % n_col]) for i in range(n_col)]
    bwd = [(b, a) for a, b in fwd]

    def row_perm(dx, k):
        return [
            (((x + dx) % n_x) * 2 + (c ^ k), x * 2 + c) for x in range(n_x) for c in range(2)
        ]

    def from_row(value, dx, k):
        return lax.ppermute(value, "row", row_perm(dx, k))

    def to_x(value, dx):
        return lax.ppermute(
            value, "row", [(x * 2 + c, ((x + dx) % n_x) * 2 + c) for x in range(n_x) for c in range(2)]
        )

    w_other = from_row(w_query, 0, 1)
    gain = jnp.concatenate([norm_gain, from_row(norm_gain, 0, 1)])

    def features_of(x):
        return jnp.concatenate(
            [
                lax.dynamic_slice_in_dim(rollouts, (x * 2 + (me_k ^ k)) * width, width, 1)
                for k in range(2)
            ],
            axis=1,
        )

    def swap_cores(parts):
        pairs = [[2 * x, 2 * x + 1] for x in range(n_x)]
        return lax.all_to_all(parts, "row", 0, 0, axis_index_groups=pairs)

    pieces = [features_of((me_x - dx) % n_x) for dx in range(1, n_x)]
    rollouts = after(rollouts, pieces)
    raw = rollouts.astype(F32)
    inverse = lax.rsqrt(jnp.sum(raw * raw, axis=1) / full_width + 1e-05)
    held = []
    for dx in range(n_x):
        if dx:
            piece, scale = from_row(pieces[dx - 1], dx, 0), from_row(inverse, dx, 0)
            piece, scale = after((piece, scale), held[0])
        else:
            piece, scale = features_of(me_x), inverse
        held.append((piece.astype(F32) * scale[:, None] * gain).astype(BF16))

    kv_head = me_c * heads // (HEADS // KV_HEADS)
    w_kv = lax.dynamic_slice_in_dim(w_keyvalue, kv_head * HEAD_DIM, HEAD_DIM, 2).reshape(width, -1)
    w_kv_other = from_row(after(w_kv, held[-1]), 0, 1)
    w_all = stack_weights(0, w_query, after(w_kv, held[-1]), None)
    w_all = stack_weights(1, w_other, w_kv_other, w_all)

    lengths, offsets, me_r, me_c = after((lengths, offsets, me_r, me_c), held[-1])
    me_x, me_k = me_r // 2, me_r % 2
    my_place = jnp.asarray(place, jnp.int32)[me_c]
    dest = order_a[(my_place + jnp.arange(n_col, dtype=jnp.int32)) % n_col]
    served = (me_x + half_x) % n_x * 2 + me_k
    row_first = lax.dynamic_slice_in_dim(lengths[:, 0], served * n_col, n_col)[dest]

    kinds = [[0]] + [[n_col - s, s] for s in range(1, half)] + [[half]]
    bases, base = [], 0
    for chunks in kinds:
        bases.append(base)
        base += len(chunks) * n_row * slots

    def positions(dep):
        lengths_now, offsets_now = after((lengths, offsets), dep)
        source = locate(lengths_now, offsets_now, slots, tokens)
        owner, slot = source // slots, source % slots
        owner_r, owner_c = owner // n_col, owner % n_col
        far = (jnp.asarray(place, jnp.int32)[owner_c] - my_place) % n_col
        d_x = (owner_r // 2 - half_x - me_x) % n_x
        member_of, base_of, size_of, last_of = ([0] * n_col for _ in range(4))
        for chunks, base in zip(kinds, bases):
            for m, q in enumerate(chunks):
                member_of[q], base_of[q], size_of[q] = m, base, len(chunks)
        for m, q in enumerate(kinds[half - 1] + kinds[half]):
            member_of[q], base_of[q], size_of[q], last_of[q] = m, bases[half - 1], 3, 1
        table = lambda values: jnp.asarray(values, jnp.int32)[far]
        core = jnp.where(table(last_of) == 1, (owner_r % 2) ^ me_k, owner_r % 2)
        place_in = (
            table(base_of)
            + ((core * table(size_of) + table(member_of)) * n_x + d_x) * slots
            + slot
        )
        return place_in.reshape(n_col, TOK_COL)[dest].reshape(tokens)

    packed, place_in = [None], [None]

    def work(g, group):
        m = len(group)
        x_type = BF16 if g == half - 1 else F32
        dep = yield
        rows = jnp.concatenate(after([block for chunk in group for block in chunk], dep))
        rows = lax.optimization_barrier(rows)
        chip = jnp.dot(rows, w_all, preferred_element_type=F32).reshape(m, n_x, slots, -1)
        sums = [
            to_x(chip[:, dx].astype(x_type), (dx + half_x) % n_x)
            for dx in range(n_x)
            if dx != half_x
        ]
        dep = yield chip
        first, chip = after((row_first, chip), dep)
        mine = attend(first, kinds[g], heads, chip, half_x, sums)
        dep = yield mine
        here = jnp.stack([mine] + [from_row(mine, dx, 0) for dx in range(1, n_x)], axis=1)
        here = after(here, dep).reshape(m * n_x * slots, -1)
        if g == half - 1:
            kept.append(here)
            yield here
            return
        if g == half:
            here = jnp.concatenate([kept[0], here])
        rows = here.shape[0]
        if g == half:
            parts = [here, from_row(here, 0, 1)]
        else:
            parts = [swap_cores(jnp.stack([here, here])).reshape(2 * rows, -1)]
        number, placed = bases[min(g, half - 1)], packed[0]
        for part in parts:
            pick = place_in[0][:, None] == number + jnp.arange(part.shape[0], dtype=jnp.int32)[None, :]
            number += part.shape[0]
            more = jnp.dot(pick.astype(BF16), part, preferred_element_type=F32)
            placed = (more if placed is None else more + placed.astype(F32)).astype(BF16)
        packed[0] = placed
        yield packed[0]

    kept = []
    running = [None] * (half + 1)
    latest = [held[-1]]

    def begin(g, group):
        running[g] = work(g, group)
        next(running[g])

    def window(arrival, groups):
        dep = (latest[0], arrival)
        for g in groups:
            dep = running[g].send(dep)
        latest[0] = dep

    ahead = [lax.ppermute(h, "col", fwd) for h in held]
    behind = [lax.ppermute(h, "col", bwd) for h in held]
    begin(0, [held])
    window(held[-1], (0,))
    last = []
    for s in range(1, half):
        begin(s, [ahead, behind])
        next_ahead, next_behind = list(ahead), list(behind)
        for part in range(2):
            dxs = range(part * half_x, (part + 1) * half_x)
            gate = latest[0] if s > 1 or part else held[-1]
            for dx in dxs:
                front, back = after((ahead[dx], behind[dx]), gate)
                if s < half - 1:
                    next_ahead[dx] = lax.ppermute(front, "col", fwd)
                    next_behind[dx] = lax.ppermute(back, "col", bwd)
                elif part == 0:
                    last.append(lax.ppermute(front, "col", fwd))
                else:
                    last.append(lax.ppermute(back, "col", bwd))
            if part == 0:
                steps = (s - 2,) if s > 1 else ()
            else:
                steps = (s - 1, s)
            window([(ahead[dx], behind[dx]) for dx in dxs], steps)
            if s == 1 and part == 0:
                place_in[0] = positions(latest[0])
            elif s == 1:
                latest[0] = (latest[0], place_in[0])
        ahead, behind = next_ahead, next_behind
    begin(half, [last])
    window(last, (half, half - 2, half - 1, half, half - 1, half))
    packed = packed[0]

    blocks = packed.reshape(n_col, TOK_COL, -1)
    cols = w_out.shape[1]
    w_parts = [w_out[:, : cols // 2], w_out[:, cols // 2 :]]

    def product(q, part, more=None):
        block = blocks[q % n_col]
        if more is not None:
            block = after(block, more)
        out = jnp.dot(block, w_parts[part], preferred_element_type=F32)
        out = lax.reduce_precision(out, 8, 7)
        return out if more is None else out + more.astype(F32)

    send_f, send_b = [None, None], [None, None]
    for q in range(half, 0, -1):
        for part in range(2):
            if q == half and part == 1:
                continue
            send_f[part] = lax.ppermute(product(q, part, send_f[part]).astype(BF16), "col", fwd)
            back = 1 - part
            send_b[back] = lax.ppermute(product(-q, back, send_b[back]).astype(BF16), "col", bwd)
    final = [
        (product(0, p) + send_f[p].astype(F32) + send_b[p].astype(F32)).astype(BF16) for p in range(2)
    ]
    return jnp.concatenate(final, axis=1)


def solution(mesh):
    in_specs = (
        P(("row", "col"), None),
        P(),
        P(),
        P("row"),
        P("row", "col"),
        P("row", None, None),
        P("col", "row"),
    )
    call = functools.partial(body, mesh.shape["row"], mesh.shape["col"])
    return jax.shard_map(call, mesh=mesh, in_specs=in_specs, out_specs=P("col", "row"), check_vma=False)
```

```python
import functools

import jax
import jax.numpy as jnp
from jax import lax
from jax.experimental import pallas as pl
from jax.experimental.pallas import tpu as pltpu
from jax.sharding import PartitionSpec as P

HEADS = 64
KV_HEADS = 8
HEAD_DIM = 128
TOK_COL = 256
F32 = jnp.float32
BF16 = jnp.bfloat16


def locate(lengths, offsets, slot_count, tokens):
    local_start = jnp.cumsum(lengths, axis=1) - lengths
    owners = lengths.shape[0]
    slot_start = jnp.arange(owners, dtype=jnp.int32)[:, None] * slot_count + local_start
    roll_offset = offsets.reshape(-1)
    roll_length = lengths.reshape(-1)
    positions = jnp.arange(tokens, dtype=jnp.int32)
    member = (
        (positions[:, None] >= roll_offset[None, :])
        & (positions[:, None] < (roll_offset + roll_length)[None, :])
    ).astype(jnp.int32)
    return jnp.sum(member * (slot_start.reshape(-1) - roll_offset)[None, :], axis=1) + positions


def attend_kernel(heads, chunks, first_ref, *refs):
    *sum_refs, out_ref = refs
    slots, columns = sum_refs[0].shape[-2:]
    total = sum_refs[0][...].reshape(slots, columns)
    for ref in sum_refs[1:]:
        total = total + ref[...].reshape(slots, columns).astype(F32)
    qkv = total.astype(BF16).astype(F32)
    width = heads * HEAD_DIM
    query = jnp.concatenate(
        [qkv[:, h * HEAD_DIM : (h + 1) * HEAD_DIM] for h in range(heads)], axis=0
    ).astype(BF16)
    keys = qkv[:, width : width + HEAD_DIM].astype(BF16)
    values = qkv[:, width + HEAD_DIM :].astype(BF16)
    chunk = jnp.int32(chunks[0])
    for m, q in enumerate(chunks):
        chunk = jnp.where(pl.program_id(0) == m, q, chunk)
    first = first_ref[chunk]
    t = lax.broadcasted_iota(jnp.int32, (slots, slots), 0)
    u = lax.broadcasted_iota(jnp.int32, (slots, slots), 1)
    allowed = (u <= t) & ((t < first) == (u < first))
    scores = lax.dot_general(
        query, keys, (((1,), (1,)), ((), ())), preferred_element_type=F32
    ) * (1.0 / HEAD_DIM**0.5)
    scores = jnp.where(allowed[None], scores.reshape(heads, slots, slots), F32(-1e30))
    top = jnp.max(scores, axis=2, keepdims=True)
    expo = jnp.exp(scores - top)
    weights = expo / jnp.sum(expo, axis=2, keepdims=True)
    weights = weights.reshape(heads * slots, slots).astype(BF16)
    out = jnp.dot(weights, values, preferred_element_type=F32)
    out_ref[0] = jnp.concatenate(
        [out[h * slots : (h + 1) * slots] for h in range(heads)], axis=1
    ).astype(BF16)


def attend(first, chunks, heads, chip_sums, which, arrived):
    count, _, slots, columns = chip_sums.shape
    out_width = heads * HEAD_DIM
    return pl.pallas_call(
        functools.partial(attend_kernel, heads, chunks),
        grid=(count,),
        in_specs=[
            pl.BlockSpec(memory_space=pltpu.SMEM),
            pl.BlockSpec((1, 1, slots, columns), lambda i: (i, which, 0, 0)),
        ]
        + [pl.BlockSpec((1, slots, columns), lambda i: (i, 0, 0)) for _ in arrived],
        out_specs=pl.BlockSpec((1, slots, out_width), lambda i: (i, 0, 0)),
        out_shape=jax.ShapeDtypeStruct((count, slots, out_width), BF16),
        compiler_params=pltpu.CompilerParams(vmem_limit_bytes=32 * 1024 * 1024),
        cost_estimate=pl.CostEstimate(flops=1000, bytes_accessed=1000, transcendentals=0),
    )(first, chip_sums, *arrived)


def stack_kernel(*refs):
    left_ref, right_ref, out_ref = refs[0], refs[1], refs[-1]
    split = left_ref.shape[1]
    out_ref[:, :split] = left_ref[...]
    out_ref[:, split:] = right_ref[...]


def stack_weights(part, left, right, old):
    rows, columns = left.shape[0], left.shape[1] + right.shape[1]
    tile = rows // 4
    wide = lambda width, base: pl.BlockSpec((tile, width), lambda i: (base + i, 0))
    kept = [] if old is None else [old]
    return pl.pallas_call(
        stack_kernel,
        grid=(4,),
        in_specs=[wide(left.shape[1], 0), wide(right.shape[1], 0)]
        + [pl.BlockSpec(memory_space=pl.ANY)] * len(kept),
        out_specs=wide(columns, 4 * part),
        out_shape=jax.ShapeDtypeStruct((2 * rows, columns), left.dtype),
        input_output_aliases={2: 0} if kept else {},
        compiler_params=pltpu.CompilerParams(vmem_limit_bytes=56 * 1024 * 1024),
        cost_estimate=pl.CostEstimate(flops=1000, bytes_accessed=1000, transcendentals=0),
    )(left, right, *kept)


def after(value, dep):
    return lax.optimization_barrier((value, dep))[0]


def ring_order(outer, inner):
    if inner == 1:
        return list(range(outer))
    if inner == 2 or outer % 2:
        order = [z * inner for z in range(outer)]
        for z in reversed(range(outer)):
            step = range(1, inner)
            order += [z * inner + y for y in (step if (outer - 1 - z) % 2 == 0 else reversed(step))]
        return order
    order = [z * inner for z in range(outer)]
    for z in reversed(range(outer)):
        step = range(1, inner)
        order += [z * inner + y for y in (step if (outer - 1 - z) % 2 == 0 else reversed(step))]
    return order


def body(n_row, n_col, rollouts, lengths, offsets, norm_gain, w_query, w_keyvalue, w_out):
    slots, full_width = rollouts.shape
    width = full_width // n_row
    tokens = TOK_COL * n_col
    n_x = n_row // 2
    half, half_x = n_col // 2, n_x // 2
    heads = w_query.shape[1] // HEAD_DIM
    order = ring_order(n_col // 2, 2) if n_col == 8 else ring_order(4, n_col // 4)
    place = [order.index(c) for c in range(n_col)]
    me_r, me_c = lax.axis_index("row"), lax.axis_index("col")
    me_x, me_k = me_r // 2, me_r % 2
    order_a = jnp.asarray(order, jnp.int32)

    fwd = [(order[i], order[(i + 1) % n_col]) for i in range(n_col)]
    bwd = [(b, a) for a, b in fwd]

    def row_perm(dx, k):
        return [
            (((x + dx) % n_x) * 2 + (c ^ k), x * 2 + c) for x in range(n_x) for c in range(2)
        ]

    def from_row(value, dx, k):
        return lax.ppermute(value, "row", row_perm(dx, k))

    def to_x(value, dx):
        return lax.ppermute(
            value, "row", [(x * 2 + c, ((x + dx) % n_x) * 2 + c) for x in range(n_x) for c in range(2)]
        )

    w_other = from_row(w_query, 0, 1)
    gain = jnp.concatenate([norm_gain, from_row(norm_gain, 0, 1)])

    def features_of(x):
        return jnp.concatenate(
            [
                lax.dynamic_slice_in_dim(rollouts, (x * 2 + (me_k ^ k)) * width, width, 1)
                for k in range(2)
            ],
            axis=1,
        )

    def swap_cores(parts):
        pairs = [[2 * x, 2 * x + 1] for x in range(n_x)]
        return lax.all_to_all(parts, "row", 0, 0, axis_index_groups=pairs)

    pieces = [features_of((me_x - dx) % n_x) for dx in range(1, n_x)]
    rollouts = after(rollouts, pieces)
    raw = rollouts.astype(F32)
    inverse = lax.rsqrt(jnp.sum(raw * raw, axis=1) / full_width + 1e-05)
    held = []
    for dx in range(n_x):
        if dx:
            piece, scale = from_row(pieces[dx - 1], dx, 0), from_row(inverse, dx, 0)
            piece, scale = after((piece, scale), held[0])
        else:
            piece, scale = features_of(me_x), inverse
        held.append((piece.astype(F32) * scale[:, None] * gain).astype(BF16))

    kv_head = me_c * heads // (HEADS // KV_HEADS)
    w_kv = lax.dynamic_slice_in_dim(w_keyvalue, kv_head * HEAD_DIM, HEAD_DIM, 2).reshape(width, -1)
    w_kv_other = from_row(after(w_kv, held[-1]), 0, 1)
    w_all = stack_weights(0, w_query, after(w_kv, held[-1]), None)
    w_all = stack_weights(1, w_other, w_kv_other, w_all)

    lengths, offsets, me_r, me_c = after((lengths, offsets, me_r, me_c), held[-1])
    me_x, me_k = me_r // 2, me_r % 2
    my_place = jnp.asarray(place, jnp.int32)[me_c]
    dest = order_a[(my_place + jnp.arange(n_col, dtype=jnp.int32)) % n_col]
    served = (me_x + half_x) % n_x * 2 + me_k
    row_first = lax.dynamic_slice_in_dim(lengths[:, 0], served * n_col, n_col)[dest]

    kinds = [[0]] + [[n_col - s, s] for s in range(1, half)] + [[half]]
    bases, base = [], 0
    for chunks in kinds:
        bases.append(base)
        base += len(chunks) * n_row * slots

    def positions(dep):
        lengths_now, offsets_now = after((lengths, offsets), dep)
        source = locate(lengths_now, offsets_now, slots, tokens)
        owner, slot = source // slots, source % slots
        owner_r, owner_c = owner // n_col, owner % n_col
        far = (jnp.asarray(place, jnp.int32)[owner_c] - my_place) % n_col
        d_x = (owner_r // 2 - half_x - me_x) % n_x
        member_of, base_of, size_of, last_of = ([0] * n_col for _ in range(4))
        for chunks, base in zip(kinds, bases):
            for m, q in enumerate(chunks):
                member_of[q], base_of[q], size_of[q] = m, base, len(chunks)
        for m, q in enumerate(kinds[half - 1] + kinds[half]):
            member_of[q], base_of[q], size_of[q], last_of[q] = m, bases[half - 1], 3, 1
        table = lambda values: jnp.asarray(values, jnp.int32)[far]
        core = jnp.where(table(last_of) == 1, (owner_r % 2) ^ me_k, owner_r % 2)
        place_in = (
            table(base_of)
            + ((core * table(size_of) + table(member_of)) * n_x + d_x) * slots
            + slot
        )
        return place_in.reshape(n_col, TOK_COL)[dest].reshape(tokens)

    packed, place_in = [None], [None]

    def place_rows(places, old, number, parts):
        placed = old
        for part in parts:
            pick = places[:, None] == number + jnp.arange(part.shape[0], dtype=jnp.int32)[None, :]
            number += part.shape[0]
            more = jnp.dot(pick.astype(BF16), part, preferred_element_type=F32)
            placed = (more if placed is None else more + placed.astype(F32)).astype(BF16)
        return placed

    def work(g, group):
        m = len(group)
        x_type = BF16 if g == half - 1 else F32
        dep = yield
        rows = jnp.concatenate(after([block for chunk in group for block in chunk], dep))
        rows = lax.optimization_barrier(rows)
        chip = jnp.dot(rows, w_all, preferred_element_type=F32).reshape(m, n_x, slots, -1)
        sums = [
            to_x(chip[:, dx].astype(x_type), (dx + half_x) % n_x)
            for dx in range(n_x)
            if dx != half_x
        ]
        dep = yield chip
        first, chip = after((row_first, chip), dep)
        mine = attend(first, kinds[g], heads, chip, half_x, sums)
        dep = yield mine
        here = jnp.stack([mine] + [from_row(mine, dx, 0) for dx in range(1, n_x)], axis=1)
        here = after(here, dep).reshape(m * n_x * slots, -1)
        if g == half - 1:
            kept.append(here)
            yield here
            return
        if g == half:
            here = jnp.concatenate([kept[0], here])
        rows = here.shape[0]
        if g == half:
            kept.append([here, from_row(here, 0, 1)])
            yield here
            return
        parts = [swap_cores(jnp.stack([here, here])).reshape(2 * rows, -1)]
        packed[0] = place_rows(place_in[0], packed[0], bases[g], parts)
        yield packed[0]

    kept = []
    running = [None] * (half + 1)
    latest = [held[-1]]

    def begin(g, group):
        running[g] = work(g, group)
        next(running[g])

    def window(arrival, groups):
        dep = (latest[0], arrival)
        for g in groups:
            dep = running[g].send(dep)
        latest[0] = dep

    ahead = [lax.ppermute(h, "col", fwd) for h in held]
    behind = [lax.ppermute(h, "col", bwd) for h in held]
    begin(0, [held])
    window(held[-1], (0,))
    last = []
    for s in range(1, half):
        begin(s, [ahead, behind])
        next_ahead, next_behind = list(ahead), list(behind)
        for part in range(2):
            dxs = range(part * half_x, (part + 1) * half_x)
            gate = latest[0] if s > 1 or part else held[-1]
            for dx in dxs:
                front, back = after((ahead[dx], behind[dx]), gate)
                if s < half - 1:
                    next_ahead[dx] = lax.ppermute(front, "col", fwd)
                    next_behind[dx] = lax.ppermute(back, "col", bwd)
                elif part == 0:
                    last.append(lax.ppermute(front, "col", fwd))
                else:
                    last.append(lax.ppermute(back, "col", bwd))
            if part == 0:
                steps = (s - 2,) if s > 1 else ()
            else:
                steps = (s - 1, s)
            window([(ahead[dx], behind[dx]) for dx in dxs], steps)
            if s == 1 and part == 0:
                place_in[0] = positions(latest[0])
            elif s == 1:
                latest[0] = (latest[0], place_in[0])
        ahead, behind = next_ahead, next_behind
    begin(half, [last])
    window(last, (half, half - 2, half - 1, half, half - 1, half))
    low, high = (half - 1) * TOK_COL, (half + 2) * TOK_COL
    early = place_rows(place_in[0][low:high], packed[0][low:high], bases[half - 1], kept[-1])
    blocks = {half - 1 + i: early[i * TOK_COL : (i + 1) * TOK_COL] for i in range(3)}

    cols = w_out.shape[1]
    w_parts = [w_out[:, : cols // 2], w_out[:, cols // 2 :]]

    def product(q, part, more=None):
        block = blocks[q % n_col]
        if more is not None:
            block = after(block, more)
        out = jnp.dot(block, w_parts[part], preferred_element_type=F32)
        out = lax.reduce_precision(out, 8, 7)
        return out if more is None else out + more.astype(F32)

    starts = {}
    for q, part in ((half, 0), (-half, 1), (half - 1, 1), (1 - half, 0)):
        starts[q, part] = product(q, part).astype(BF16)
    outside = lambda rows: jnp.concatenate([rows[high:], rows[:low]])
    parts = after(kept[-1], list(starts.values()))
    late = place_rows(outside(place_in[0]), outside(packed[0]), bases[half - 1], parts)
    for i in range(n_col - 3):
        blocks[(half + 2 + i) % n_col] = late[i * TOK_COL : (i + 1) * TOK_COL]

    send_f, send_b = [None, None], [None, None]
    for q in range(half, 0, -1):
        for part in range(2):
            if q == half and part == 1:
                continue
            back = 1 - part
            value = starts.get((q, part))
            if value is None:
                value = product(q, part, send_f[part]).astype(BF16)
            send_f[part] = lax.ppermute(value, "col", fwd)
            value = starts.get((-q, back))
            if value is None:
                value = product(-q, back, send_b[back]).astype(BF16)
            send_b[back] = lax.ppermute(value, "col", bwd)
    final = [
        (product(0, p) + send_f[p].astype(F32) + send_b[p].astype(F32)).astype(BF16) for p in range(2)
    ]
    return jnp.concatenate(final, axis=1)


def solution(mesh):
    in_specs = (
        P(("row", "col"), None),
        P(),
        P(),
        P("row"),
        P("row", "col"),
        P("row", None, None),
        P("col", "row"),
    )
    call = functools.partial(body, mesh.shape["row"], mesh.shape["col"])
    return jax.shard_map(call, mesh=mesh, in_specs=in_specs, out_specs=P("col", "row"), check_vma=False)
```
